128 devices in a mesh: wide: 16 (over z, x_hi, core), narrow: 8 (over y, x_lo).
Axes of the slice: x: 4 (x_hi: 2, x_lo: 2; x = x_hi * 2 + x_lo), y: 4, z: 4, core: 2. Of those that a mesh axis runs over, the one named last changes fastest.
Arguments:
- grav_levels: float32 [4, 512, 256, 128], P(None, 'wide', 'narrow'), may hold values from -6 to 6
- grav_step: float32 [4, 512, 256, 128], P(None, 'wide', 'narrow'), may hold values from -6 to 6
- seis_levels: float32 [4, 512, 256, 128], P(None, None, ('wide', 'narrow')), may hold values from -6 to 6
- seis_step: float32 [4, 512, 256, 128], P(None, None, ('wide', 'narrow')), may hold values from -6 to 6
- unit_labels: int32 [4], replicated, may hold values from 0 to 4
- dens_index: int32 [5], replicated, may hold values from 0 to 7
- vel_index: int32 [5], replicated, may hold values from 0 to 7
- dens_table: float32 [8], replicated, may hold values from 0.5 to 2
- vel_table: float32 [8], replicated, may hold values from 0.5 to 2
Outputs:
- grav_gradient: float32 [4, 512, 256, 128], P(None, 'wide', 'narrow')
- grav_curvature: float32 [4, 512, 256, 128], P(None, 'wide', 'narrow')
- seis_gradient: float32 [4, 512, 256, 128], P(None, None, ('wide', 'narrow'))
- seis_curvature: float32 [4, 512, 256, 128], P(None, None, ('wide', 'narrow'))
The draws below stay inside these ranges and needn't reach their ends.
All inputs are finite; a program needn't handle non-finite values.
Results may differ from the reference program's by a relative error of at most 0.0003.
Values sent between devices are 32-bit elements; how exact they have to be, the bound alone decides.
A program may use at most 128 MiB of HBM per device.

```python
import math
import jax
import jax.numpy as jnp

NZ = 128
LEVELS = 4
UNITS = 5
TABLE = 8
NX = 512
NY = 256


def place_ends(array, rng, least, top_value):
    dims = array.shape
    spot = [jax.random.randint(jax.random.fold_in(rng, axis), (), 0, dims[axis]) for axis in range(len(dims))]
    array = array.at[tuple(spot)].set(least)
    longest = dims.index(max(dims))
    spot[longest] = (spot[longest] + 1) % dims[longest]
    return array.at[tuple(spot)].set(top_value)


def level_of(own_key, extent, cuts, low, top_value):
    factor_of = 1.0
    for axis_at, shards_of in cuts:
        steps = jax.random.uniform(jax.random.fold_in(jax.random.fold_in(own_key, 6), axis_at), (shards_of,), jnp.float32, low / len(cuts), top_value / len(cuts))
        factor_of = factor_of * jnp.repeat(jnp.exp(steps), extent[axis_at] // shards_of).reshape((-1,) + (1,) * (len(extent) - 1 - axis_at))
    return factor_of


def noise(key, dims, spread, limit, pieces=(), kind=jnp.bfloat16):
    entries = jax.random.normal(key, dims, jnp.float32) * spread
    if len(pieces) > 0:
        entries = level_of(key, dims, pieces, -0.22, 0.18) * entries
    return jnp.clip(entries, min=-limit, max=limit).astype(kind)


def setup_inputs(seed: int = 0) -> dict:
    streams_of = jax.random.split(jax.random.key(seed), 10)
    grav_levels = noise(streams_of[0], (LEVELS, NX, NY, NZ), 1.0, 6.0, ((1, 16), (2, 8)), jnp.float32)
    grav_step = noise(streams_of[1], (LEVELS, NX, NY, NZ), 1.0, 6.0, ((1, 16), (2, 8)), jnp.float32)
    seis_levels = noise(streams_of[2], (LEVELS, NX, NY, NZ), 1.0, 6.0, ((2, 128),), jnp.float32)
    seis_step = noise(streams_of[3], (LEVELS, NX, NY, NZ), 1.0, 6.0, ((2, 128),), jnp.float32)
    unit_labels = place_ends(jax.random.randint(streams_of[4], (LEVELS,), 0, UNITS), jax.random.fold_in(streams_of[4], 1), 0, UNITS - 1).astype(jnp.int32)
    dens_index = place_ends(jax.random.randint(streams_of[5], (UNITS,), 0, TABLE), jax.random.fold_in(streams_of[5], 1), 0, TABLE - 1).astype(jnp.int32)
    vel_index = place_ends(jax.random.randint(streams_of[6], (UNITS,), 0, TABLE), jax.random.fold_in(streams_of[6], 1), 0, TABLE - 1).astype(jnp.int32)
    dens_table = jnp.clip(jnp.exp(jax.random.uniform(streams_of[7], (TABLE,), jnp.float32, math.log(0.5), math.log(2.0))), 0.5, 2.0)
    vel_table = jnp.clip(jnp.exp(jax.random.uniform(streams_of[8], (TABLE,), jnp.float32, math.log(0.5), math.log(2.0))), 0.5, 2.0)
    return {"grav_levels": grav_levels, "grav_step": grav_step, "seis_levels": seis_levels, "seis_step": seis_step, "unit_labels": unit_labels, "dens_index": dens_index, "vel_index": vel_index, "dens_table": dens_table, "vel_table": vel_table}


smooth_width = 1.0


def lookup_coeffs(unit_labels, table_index, values_table):
    table_slots = jnp.arange(values_table.shape[0], dtype=jnp.int32)
    per_unit = jnp.sum(jnp.where(table_index[:, None] == table_slots[None, :], values_table[None, :], 0.0), axis=1)
    unit_slots = jnp.arange(table_index.shape[0], dtype=jnp.int32)
    return jnp.sum(jnp.where(unit_labels[:, None] == unit_slots[None, :], per_unit[None, :], 0.0), axis=1)


def heaviside(level_field):
    return 0.5 * (1.0 + jnp.tanh(level_field / smooth_width))


def heaviside_slope(level_field):
    tanh_value = jnp.tanh(level_field / smooth_width)
    return (0.5 / smooth_width) * (1.0 - tanh_value * tanh_value)


def mix_levels(levels, coeffs):
    summed = coeffs[0] * heaviside(levels[0])
    for level in range(1, levels.shape[0]):
        summed = summed + coeffs[level] * heaviside(levels[level])
    return summed


def mix_steps(levels, directions, coeffs):
    summed = (coeffs[0] * heaviside_slope(levels[0])) * directions[0]
    for level in range(1, levels.shape[0]):
        summed = summed + (coeffs[level] * heaviside_slope(levels[level])) * directions[level]
    return summed


def chain_rule(levels, coeffs, force):
    return jnp.stack([(coeffs[level] * heaviside_slope(levels[level])) * force for level in range(levels.shape[0])])


def cross_product(first_vec, second_vec):
    return (first_vec[1] * second_vec[2] - first_vec[2] * second_vec[1],
            first_vec[2] * second_vec[0] - first_vec[0] * second_vec[2],
            first_vec[0] * second_vec[1] - first_vec[1] * second_vec[0])


def inner_gradient(padded):
    depth_pad = jnp.pad(padded, ((0, 0), (0, 0), (1, 1)))
    grad_x = (padded[2:, 1:-1] - padded[:-2, 1:-1]) * 0.5
    grad_y = (padded[1:-1, 2:] - padded[1:-1, :-2]) * 0.5
    grad_z = (depth_pad[1:-1, 1:-1, 2:] - depth_pad[1:-1, 1:-1, :-2]) * 0.5
    return (grad_x, grad_y, grad_z)


def inner_adjoint(vector):
    depth_pad = jnp.pad(vector[2], ((0, 0), (0, 0), (1, 1)))
    along_x = (vector[0][:-2, 1:-1] - vector[0][2:, 1:-1]) * 0.5
    along_y = (vector[1][1:-1, :-2] - vector[1][1:-1, 2:]) * 0.5
    along_z = (depth_pad[1:-1, 1:-1, :-2] - depth_pad[1:-1, 1:-1, 2:]) * 0.5
    return along_x + along_y + along_z


def coupling_vectors(dens_grad, vel_grad, dchange_grad, vchange_grad):
    cross_vec = cross_product(dens_grad, vel_grad)
    change = tuple(first_term + second_term for first_term, second_term in
                   zip(cross_product(dchange_grad, vel_grad), cross_product(dens_grad, vchange_grad)))
    return (cross_product(vel_grad, cross_vec), cross_product(cross_vec, dens_grad),
            cross_product(vel_grad, change), cross_product(change, dens_grad))


def gradient(scalar_field):
    return inner_gradient(jnp.pad(scalar_field, ((1, 1), (1, 1), (0, 0))))


def adjoint(vector):
    return inner_adjoint(tuple(jnp.pad(component, ((1, 1), (1, 1), (0, 0))) for component in vector))


def reference(grav_levels, grav_step, seis_levels, seis_step, unit_labels, dens_index, vel_index, dens_table, vel_table):
    dens_coeff = lookup_coeffs(unit_labels, dens_index, dens_table)
    vel_coeff = lookup_coeffs(unit_labels, vel_index, vel_table)
    density = mix_levels(grav_levels, dens_coeff)
    velocity = mix_levels(seis_levels, vel_coeff)
    dens_change = mix_steps(grav_levels, grav_step, dens_coeff)
    vel_change = mix_steps(seis_levels, seis_step, vel_coeff)
    gradients = [gradient(item) for item in (density, velocity, dens_change, vel_change)]
    vectors = coupling_vectors(*gradients)
    dens_force, vel_force, dens_curvature, vel_curvature = [adjoint(vector) for vector in vectors]
    grav_gradient = chain_rule(grav_levels, dens_coeff, dens_force)
    grav_curvature = chain_rule(grav_levels, dens_coeff, dens_curvature)
    seis_gradient = chain_rule(seis_levels, vel_coeff, vel_force)
    seis_curvature = chain_rule(seis_levels, vel_coeff, vel_curvature)
    return (grav_gradient, grav_curvature, seis_gradient, seis_curvature)
```

```python
import functools

import jax
import jax.numpy as jnp
from jax import lax
from jax.experimental import pallas as pl
from jax.experimental.pallas import tpu as pltpu
from jax.sharding import PartitionSpec as P

MESH = pl.DeviceIdType.MESH
NX = 32
NY = 32
PITCH = NX + 4
MSG = 2 * PITCH
COLS = (NY + 4) * PITCH
PAD = 8


def both(one, other):
    return jnp.logical_and(one, other)


class Place:
    def __init__(self):
        self.w = lax.axis_index("wide")
        self.n = lax.axis_index("narrow")
        self.z = self.w // 4
        self.xh = (self.w // 2) % 2
        self.c = self.w % 2
        self.y = self.n // 2
        self.xl = self.n % 2
        self.x = self.xh * 2 + self.xl
        self.mid = (self.xh + self.xl) % 2

    @staticmethod
    def device(z, xh, c, y, xl):
        return (z * 4 + xh * 2 + c, y * 2 + xl)

    def is_me(self, device):
        return both(device[0] == self.w, device[1] == self.n)

    def across(self, a):
        return self.x + (1 - self.mid) * a * (3 - 2 * self.x)

    def first_leg(self, dz, a, c2):
        z2 = (self.z + dz) % 4
        xr = self.across(a)
        xh2 = self.mid * a + (1 - self.mid) * (xr // 2)
        relay = self.device(z2, xr // 2, self.c, self.y, xr % 2)
        return z2 * 4 + xh2 * 2 + c2, relay, self.z * 4 + a * 2 + c2, self.is_me(relay)

    def second_leg(self, dz, a, c2):
        zs = (self.z + 4 - dz) % 4
        xs = self.across(a)
        xh2 = self.mid * a + (1 - self.mid) * self.xh
        brick = self.device(self.z, xh2, c2, zs, xs // 2)
        return zs * 4 + a * 2 + c2, brick, self.c * 8 + self.y * 2 + xs % 2

    def slab(self, pair):
        return (self.n * 2 + pair // 8, pair % 8)


def coeffs(labels, index, table):
    return [table[index[labels[level]]] for level in range(4)]


def depth_change(field):
    lane = lax.broadcasted_iota(jnp.int32, field.shape, field.ndim - 1)
    up = jnp.where(lane == 127, 0.0, pltpu.roll(field, 127, field.ndim - 1))
    down = jnp.where(lane == 0, 0.0, pltpu.roll(field, 1, field.ndim - 1))
    return up - down


def cross(p, q):
    return (p[1] * q[2] - p[2] * q[1], p[2] * q[0] - p[0] * q[2], p[0] * q[1] - p[1] * q[0])


def cross_first(p, q):
    return p[1] * q[2] - p[2] * q[1]


def coupled(curvature, grads):
    if curvature:
        dens, vel, dchange, vchange = grads
        mixed = tuple(s + t for s, t in zip(cross(dchange, vel), cross(dens, vchange)))
    else:
        dens, vel = grads
        mixed = cross(dens, vel)
    return dens, vel, mixed


def forces_kernel(
    grav_levels,
    grav_step,
    seis_levels,
    seis_step,
    labels,
    dens_index,
    vel_index,
    dens_table,
    vel_table,
    dens_out,
    vel_out,
    gl,
    gs,
    sl,
    st,
    sb,
    hb,
    rb,
    db,
    xs,
    xr,
    q1e,
    q1s,
    q2s,
    acc,
    df,
    rs,
    rv,
    load_sem,
    leg1_send,
    leg1_recv,
    leg2_send,
    leg2_recv,
    xh_send,
    xh_recv,
    yd_send,
    yd_recv,
    yv_send,
    yv_recv,
    ret_send,
    ret_recv,
):
    me = Place()
    slab_rows = seis_levels.shape[1]

    loads = []
    for number, (source, target) in enumerate(
        [
            (seis_levels, sl.at[:, pl.ds(PAD, slab_rows), :]),
            (seis_step, st.at[:, pl.ds(PAD, slab_rows), :]),
            (grav_levels, gl),
            (grav_step, gs),
        ]
    ):
        copy = pltpu.make_async_copy(source, target, load_sem.at[number])
        copy.start()
        loads.append(copy)

    barrier = pltpu.get_barrier_semaphore()

    def greet(device):
        pl.semaphore_signal(barrier, inc=1, device_id=device, device_id_type=MESH)

    def greet_first(i, _):
        device = me.first_leg(i // 2, i % 2, 0)[1]

        @pl.when(jnp.logical_not(me.is_me(device)))
        def _():
            greet(device)

        return 0

    lax.fori_loop(0, 8, greet_first, 0)

    def greet_second(i, _):
        y2, c2, far = i // 4, (i // 2) % 2, i % 2
        xr_mid = 1 + me.xl
        xr_end = 3 * me.xh
        x2 = far * xr_end + (1 - far) * xr_mid
        device = me.device(me.z, x2 // 2, c2, y2, x2 % 2)

        @pl.when(jnp.logical_not(me.is_me(device)))
        def _():
            greet(device)

        return 0

    lax.fori_loop(0, 16, greet_second, 0)

    def greet_return(i, _):
        device = (i, me.z * 2 + me.xh)

        @pl.when(jnp.logical_not(me.is_me(device)))
        def _():
            greet(device)

        return 0

    lax.fori_loop(0, 16, greet_return, 0)
    has_low_x, has_high_x = me.w > 0, me.w < 15
    has_low_y, has_high_y = me.n > 0, me.n < 7
    low_x, high_x = (me.w - 1, me.n), (me.w + 1, me.n)
    low_y, high_y = (me.w, me.n - 1), (me.w, me.n + 1)
    sides = ((has_low_x, low_x), (has_high_x, high_x), (has_low_y, low_y), (has_high_y, high_y))
    for here, device in sides:

        @pl.when(here)
        def _():
            greet(device)

    def not_me(device):
        return 1 - me.is_me(device).astype(jnp.int32)

    expected = 0
    for here, _ in sides:
        expected = expected + here.astype(jnp.int32)
    for i in range(8):
        expected = expected + not_me(me.first_leg(i // 2, i % 2, 0)[1])
    for i in range(16):
        expected = expected + not_me(me.second_leg(i // 4, (i // 2) % 2, i % 2)[1])
        expected = expected + not_me(me.slab(i))

    dens_coeff = [0.5 * v for v in coeffs(labels, dens_index, dens_table)]
    vel_coeff = [0.5 * v for v in coeffs(labels, vel_index, vel_table)]

    def remote(source, target, send, recv, device):
        return pltpu.make_async_remote_copy(
            src_ref=source,
            dst_ref=target,
            send_sem=send,
            recv_sem=recv,
            device_id=device,
            device_id_type=MESH,
        )

    def start_any(source, target, send, recv, device):
        mine = me.is_me(device)

        @pl.when(mine)
        def _():
            pltpu.make_async_copy(source, target, recv).start()

        @pl.when(jnp.logical_not(mine))
        def _():
            remote(source, target, send, recv, device).start()

    def await_send(source, send, device):
        @pl.when(jnp.logical_not(me.is_me(device)))
        def _():
            remote(source, source, send, send, device).wait_send()

    def await_recv(target, recv):
        pltpu.make_async_copy(target, target, recv).wait()

    def message(field, slot):
        return sb.at[field, slot]

    def brick_slot(field, slot):
        return rb.at[field, pl.ds(pl.multiple_of((slot + 1) * MSG, 8), MSG), :]

    def route(i):
        dz, a, c2 = i // 4, (i // 2) % 2, i % 2
        return dz, a, c2

    def leg_two(field, i, source, finish=False):
        dz, a, c2 = route(i)
        slot, brick, there = me.second_leg(dz, a, c2)
        if finish:
            await_send(source, leg2_send.at[field, slot], brick)
        else:
            start_any(
                source,
                brick_slot(field, there),
                leg2_send.at[field, slot],
                leg2_recv.at[field, there],
                brick,
            )

    def send_slabs(field):
        def one(i, _):
            dz, a, c2 = route(i)
            block, relay, slot, stays = me.first_leg(dz, a, c2)
            x_at = block * NX - 2 + lax.broadcasted_iota(jnp.int32, (PITCH, 128), 0)
            inside = both(x_at >= 0, x_at < slab_rows // 2)
            for column in range(2):
                rows = pl.ds(block * 2 * NX + PAD - 4 + column, PITCH, stride=2)
                total = None
                for level in range(4):
                    t = jnp.tanh(sl[level, rows, :])
                    if field == 0:
                        term = vel_coeff[level] * (1.0 + t)
                    else:
                        term = (vel_coeff[level] * (1.0 - t * t)) * st[level, rows, :]
                    total = term if total is None else total + term
                sb[field, block, pl.ds(column * PITCH, PITCH), :] = jnp.where(inside, total, 0.0)

            @pl.when(stays)
            def _():
                leg_two(field, i, message(field, block))

            @pl.when(jnp.logical_not(stays))
            def _():
                remote(
                    message(field, block),
                    hb.at[field, slot],
                    leg1_send.at[field, block],
                    leg1_recv.at[field, slot],
                    relay,
                ).start()

            return 0

        lax.fori_loop(0, 16, one, 0)

    def relay_slabs(field):
        def one(i, _):
            dz, a, c2 = route(i)
            stays = me.first_leg(dz, a, c2)[3]
            slot = me.second_leg(dz, a, c2)[0]

            @pl.when(jnp.logical_not(stays))
            def _():
                await_recv(hb.at[field, slot], leg1_recv.at[field, slot])
                leg_two(field, i, hb.at[field, slot])

            return 0

        lax.fori_loop(0, 16, one, 0)

    loads[0].wait()
    pl.semaphore_wait(barrier, expected)
    send_slabs(0)
    loads[1].wait()
    send_slabs(1)

    loads[2].wait()
    loads[3].wait()

    def dens_row(x):
        dens, change = None, None
        for level in range(4):
            t = jnp.tanh(gl[level, x])
            term = dens_coeff[level] * (1.0 + t)
            slope = (dens_coeff[level] * (1.0 - t * t)) * gs[level, x]
            dens = term if dens is None else dens + term
            change = slope if change is None else change + slope
        rows = pl.ds(2 * PITCH + 2 + x, NY, stride=PITCH)
        db[0, rows, :] = dens
        db[1, rows, :] = change
        return dens, change

    def edge_row(k, _):
        side, row = k // 2, k % 2
        dens, change = dens_row(side * (NX - 2) + row)
        xs[side, pl.ds(pl.multiple_of(row * NY, 8), NY), :] = dens
        xs[side, pl.ds(pl.multiple_of((2 + row) * NY, 8), NY), :] = change
        return 0

    lax.fori_loop(0, 4, edge_row, 0)

    def x_halo(side):
        return remote(
            xs.at[side],
            xr.at[1 - side],
            xh_send.at[side],
            xh_recv.at[1 - side],
            (low_x, high_x)[side],
        )

    for side in range(2):

        @pl.when(sides[side][0])
        def _():
            x_halo(side).start()

    def inner_row(x, _):
        dens_row(x)
        return 0

    lax.fori_loop(2, NX - 2, inner_row, 0)

    relay_slabs(0)

    for side in range(2):
        rows = pl.ds(0, 2 * NY * 2)

        @pl.when(sides[side][0])
        def _():
            await_recv(xr.at[side], xh_recv.at[side])

        @pl.when(jnp.logical_not(sides[side][0]))
        def _():
            xr[side] = jnp.zeros(xr.shape[1:], jnp.float32)

        for field in range(2):
            for row in range(2):
                db[field, pl.ds(2 * PITCH + side * (NX + 2) + row, NY, stride=PITCH), :] = xr[
                    side, pl.ds((field * 2 + row) * NY, NY), :
                ]

    def y_halo(ref, send, recv, field, side):
        source = ref.at[field, pl.ds((2 + side * (NY - 2)) * PITCH, MSG), :]
        target = ref.at[field, pl.ds((1 - side) * (NY + 2) * PITCH, MSG), :]
        return remote(
            source, target, send.at[field, side], recv.at[field, 1 - side], (low_y, high_y)[side]
        )

    def y_halo_start(ref, send, recv, field):
        for side in range(2):

            @pl.when(sides[2 + side][0])
            def _():
                y_halo(ref, send, recv, field, side).start()

            @pl.when(jnp.logical_not(sides[2 + side][0]))
            def _():
                ref[field, pl.ds(side * (NY + 2) * PITCH, MSG), :] = jnp.zeros(
                    (MSG, 128), jnp.float32
                )

    def y_halo_recv(ref, send, recv, field):
        for side in range(2):

            @pl.when(sides[2 + side][0])
            def _():
                await_recv(
                    ref.at[field, pl.ds(side * (NY + 2) * PITCH, MSG), :], recv.at[field, side]
                )

    def y_halo_sent(ref, send, recv, field):
        for side in range(2):

            @pl.when(sides[2 + side][0])
            def _():
                y_halo(ref, send, recv, field, side).wait_send()

    for field in range(2):
        y_halo_start(db, yd_send, yd_recv, field)

    relay_slabs(1)

    def arrive(field):
        for slot in (0, 15):
            await_recv(brick_slot(field, slot), leg2_recv.at[field, slot])
        y_halo_start(rb, yv_send, yv_recv, field)

        def one(slot, _):
            await_recv(brick_slot(field, slot), leg2_recv.at[field, slot])
            return 0

        lax.fori_loop(1, 15, one, 0)

    arrive(0)
    for field in range(2):
        y_halo_recv(db, yd_send, yd_recv, field)
    y_halo_recv(rb, yv_send, yv_recv, 0)

    def gradient(ref, field, yy):
        def at(column, x):
            return ref[field, pl.ds(column * PITCH + 2 + x, NX), :]

        return (
            at(yy, 1) - at(yy, -1),
            at(yy + 1, 0) - at(yy - 1, 0),
            depth_change(at(yy, 0)),
        )

    def edge_gradient(ref, field, x):
        def at(dy, x):
            return ref[field, pl.ds((2 + dy) * PITCH + 2 + x, NY, stride=PITCH), :]

        return (at(0, x + 1) - at(0, x - 1), at(1, x) - at(-1, x), depth_change(at(0, x)))

    def compute(field):
        which = [(db, 0), (rb, 0), (db, 1), (rb, 1)][: 2 + 2 * field]

        for side in range(2):
            x = (-1, NX)[side]
            dens, vel, mixed = coupled(field, [edge_gradient(r, f, x) for r, f in which])
            keep = sides[side][0].astype(jnp.float32)
            q1e[0, side] = cross_first(vel, mixed) * keep
            q1e[1, side] = cross_first(mixed, dens) * keep

        def column(yy):
            dens, vel, mixed = coupled(field, [gradient(r, f, yy) for r, f in which])
            outside = jnp.logical_or(
                both(yy == 1, me.n == 0), both(yy == NY + 2, me.n == 7)
            )
            keep = 1.0 - outside.astype(jnp.float32)
            y = jnp.clip(yy - 2, 0, NY - 1)
            for out, q in enumerate((cross(vel, mixed), cross(mixed, dens))):
                q1s[out, pl.ds(8, NX), :] = q[0]
                q1s[out, pl.ds(7, 1), :] = q1e[out, 0, pl.ds(y, 1), :]
                q1s[out, pl.ds(8 + NX, 1), :] = q1e[out, 1, pl.ds(y, 1), :]
                along_x = q1s[out, pl.ds(7, NX), :] - q1s[out, pl.ds(9, NX), :]
                q2s[out, yy] = q[1] * keep
                acc[out, yy] = along_x - depth_change(q[2])

        column(1)
        column(2)

        def pair(p, _):
            for half in range(2):
                yy = 2 * p + 2 + half
                column(yy + 1)
                df[field, pl.ds(pl.multiple_of((yy - 2) * NX, 8), NX), :] = acc[0, yy] + (
                    q2s[0, yy - 1] - q2s[0, yy + 1]
                )
                rs[field, p, pl.ds(half * NX, NX), :] = acc[1, yy] + (
                    q2s[1, yy - 1] - q2s[1, yy + 1]
                )
            start_any(
                rs.at[field, p],
                rv.at[field, me.w],
                ret_send.at[field, p],
                ret_recv.at[field, me.w],
                me.slab(p),
            )
            return 0

        lax.fori_loop(0, 16, pair, 0)

    compute(0)
    arrive(1)
    y_halo_recv(rb, yv_send, yv_recv, 1)
    compute(1)

    for field in range(2):

        def turn(x, _):
            dens_out[field, x] = df[field, pl.ds(x, NY, stride=NX), :]
            return 0

        lax.fori_loop(0, NX, turn, 0)

    for field in range(2):

        def finish(block, _):
            await_recv(rv.at[field, block], ret_recv.at[field, block])
            for half in range(2):
                vel_out[field, pl.ds(block * 2 * NX + half, NX, stride=2), :] = rv[
                    field, block, pl.ds(half * NX, NX), :
                ]
            return 0

        lax.fori_loop(0, 16, finish, 0)

    for side in range(2):

        @pl.when(sides[side][0])
        def _():
            x_halo(side).wait_send()

    for field in range(2):
        y_halo_sent(db, yd_send, yd_recv, field)
        y_halo_sent(rb, yv_send, yv_recv, field)

        def sent(i, _):
            dz, a, c2 = route(i)
            block, relay, slot, stays = me.first_leg(dz, a, c2)

            @pl.when(jnp.logical_not(stays))
            def _():
                remote(
                    message(field, block),
                    message(field, block),
                    leg1_send.at[field, block],
                    leg1_send.at[field, block],
                    relay,
                ).wait_send()

            leg_two(field, i, hb.at[field, 0], finish=True)
            await_send(rs.at[field, 0], ret_send.at[field, i], me.slab(i))
            return 0

        lax.fori_loop(0, 16, sent, 0)


def chain_kernel(
    labels,
    dens_index,
    vel_index,
    dens_table,
    vel_table,
    grav_levels,
    seis_levels,
    dens_force,
    vel_force,
    grav_gradient,
    grav_curvature,
    seis_gradient,
    seis_curvature,
):
    for levels, force, index, table, outs in (
        (grav_levels, dens_force, dens_index, dens_table, (grav_gradient, grav_curvature)),
        (seis_levels, vel_force, vel_index, vel_table, (seis_gradient, seis_curvature)),
    ):
        scales = [v * (0.5 / 16.0) for v in coeffs(labels, index, table)]
        for level in range(4):
            t = jnp.tanh(levels[level])
            slope = scales[level] * (1.0 - t * t)
            for number in range(2):
                outs[number][level] = slope * force[number]


def shards(
    grav_levels,
    grav_step,
    seis_levels,
    seis_step,
    unit_labels,
    dens_index,
    vel_index,
    dens_table,
    vel_table,
):
    levels, nx, ny, nz = grav_levels.shape
    slab_x, slab_y = seis_levels.shape[1:3]
    rows = slab_x * slab_y
    seis_rows = seis_levels.reshape(levels, rows, nz)
    step_rows = seis_step.reshape(levels, rows, nz)
    tables = (unit_labels, dens_index, vel_index, dens_table, vel_table)
    smem = pl.BlockSpec(memory_space=pltpu.SMEM)
    hbm = pl.BlockSpec(memory_space=pl.ANY)
    vmem = pl.BlockSpec(memory_space=pltpu.VMEM)
    f32 = jnp.float32
    dma = pltpu.SemaphoreType.DMA
    dens_force, vel_force = pl.pallas_call(
        forces_kernel,
        out_shape=(
            jax.ShapeDtypeStruct((2, nx, ny, nz), f32),
            jax.ShapeDtypeStruct((2, rows, nz), f32),
        ),
        in_specs=[hbm] * 4 + [smem] * 5,
        out_specs=(vmem, vmem),
        scratch_shapes=[
            pltpu.VMEM((levels, nx, ny, nz), f32),
            pltpu.VMEM((levels, nx, ny, nz), f32),
            pltpu.VMEM((levels, rows + 4 * PAD, nz), f32),
            pltpu.VMEM((levels, rows + 4 * PAD, nz), f32),
            pltpu.VMEM((2, 16, MSG, nz), f32),
            pltpu.VMEM((2, 16, MSG, nz), f32),
            pltpu.VMEM((2, COLS, nz), f32),
            pltpu.VMEM((2, COLS, nz), f32),
            pltpu.VMEM((2, 4 * NY, nz), f32),
            pltpu.VMEM((2, 4 * NY, nz), f32),
            pltpu.VMEM((2, 2, NY, nz), f32),
            pltpu.VMEM((2, NX + 16, nz), f32),
            pltpu.VMEM((2, NY + 4, NX, nz), f32),
            pltpu.VMEM((2, NY + 4, NX, nz), f32),
            pltpu.VMEM((2, NY * NX, nz), f32),
            pltpu.VMEM((2, 16, 2 * NX, nz), f32),
            pltpu.VMEM((2, 16, 2 * NX, nz), f32),
            dma((4,)),
            dma((2, 16)),
            dma((2, 16)),
            dma((2, 16)),
            dma((2, 16)),
            dma((2,)),
            dma((2,)),
            dma((2, 2)),
            dma((2, 2)),
            dma((2, 2)),
            dma((2, 2)),
            dma((2, 16)),
            dma((2, 16)),
        ],
        compiler_params=pltpu.CompilerParams(
            collective_id=0, has_side_effects=True, vmem_limit_bytes=40 << 20
        ),
        name="forces",
    )(grav_levels, grav_step, seis_rows, step_rows, *tables)

    steps = 8
    brick = pl.BlockSpec((levels, nx // steps, ny, nz), lambda i: (0, i, 0, 0))
    slab = pl.BlockSpec((levels, rows // steps, nz), lambda i: (0, i, 0))
    brick_force = pl.BlockSpec((2, nx // steps, ny, nz), lambda i: (0, i, 0, 0))
    slab_force = pl.BlockSpec((2, rows // steps, nz), lambda i: (0, i, 0))
    brick_shape = jax.ShapeDtypeStruct(grav_levels.shape, f32)
    slab_shape = jax.ShapeDtypeStruct(seis_rows.shape, f32)
    outs = pl.pallas_call(
        chain_kernel,
        grid=(steps,),
        out_shape=(brick_shape, brick_shape, slab_shape, slab_shape),
        in_specs=[smem] * 5 + [brick, slab, brick_force, slab_force],
        out_specs=(brick, brick, slab, slab),
        compiler_params=pltpu.CompilerParams(vmem_limit_bytes=32 << 20),
        name="chain",
    )(*tables, grav_levels, seis_rows, dens_force, vel_force)
    return (
        outs[0],
        outs[1],
        outs[2].reshape(seis_levels.shape),
        outs[3].reshape(seis_levels.shape),
    )


def solution(mesh):
    placed = (
        P(None, "wide", "narrow", None),
        P(None, "wide", "narrow", None),
        P(None, None, ("wide", "narrow"), None),
        P(None, None, ("wide", "narrow"), None),
        P(),
        P(),
        P(),
        P(),
        P(),
    )
    return jax.shard_map(
        shards,
        mesh=mesh,
        in_specs=placed,
        out_specs=placed[:4],
        check_vma=False,
    )
```

```python
import functools

import jax
import jax.numpy as jnp
from jax import lax
from jax.experimental import pallas as pl
from jax.experimental.pallas import tpu as pltpu
from jax.sharding import PartitionSpec as P

MESH = pl.DeviceIdType.MESH
NX = 32
NY = 32
PITCH = NX + 4
MSG = 2 * PITCH
COLS = (NY + 4) * PITCH
PAD = 8


def both(one, other):
    return jnp.logical_and(one, other)


class Place:
    def __init__(self):
        self.w = lax.axis_index("wide")
        self.n = lax.axis_index("narrow")
        self.z = self.w // 4
        self.xh = (self.w // 2) % 2
        self.c = self.w % 2
        self.y = self.n // 2
        self.xl = self.n % 2
        self.x = self.xh * 2 + self.xl
        self.mid = (self.xh + self.xl) % 2

    @staticmethod
    def device(z, xh, c, y, xl):
        return (z * 4 + xh * 2 + c, y * 2 + xl)

    def is_me(self, device):
        return both(device[0] == self.w, device[1] == self.n)

    def across(self, a):
        return self.x + (1 - self.mid) * a * (3 - 2 * self.x)

    def first_leg(self, dz, a, c2):
        z2 = (self.z + dz) % 4
        xr = self.across(a)
        xh2 = self.mid * a + (1 - self.mid) * (xr // 2)
        relay = self.device(z2, xr // 2, self.c, self.y, xr % 2)
        return z2 * 4 + xh2 * 2 + c2, relay, self.z * 4 + a * 2 + c2, self.is_me(relay)

    def second_leg(self, dz, a, c2):
        zs = (self.z + 4 - dz) % 4
        xs = self.across(a)
        xh2 = self.mid * a + (1 - self.mid) * self.xh
        brick = self.device(self.z, xh2, c2, zs, xs // 2)
        return zs * 4 + a * 2 + c2, brick, self.c * 8 + self.y * 2 + xs % 2

    def slab(self, pair):
        return (self.n * 2 + pair // 8, pair % 8)


def coeffs(labels, index, table):
    return [table[index[labels[level]]] for level in range(4)]


def depth_change(field):
    lane = lax.broadcasted_iota(jnp.int32, field.shape, field.ndim - 1)
    up = jnp.where(lane == 127, 0.0, pltpu.roll(field, 127, field.ndim - 1))
    down = jnp.where(lane == 0, 0.0, pltpu.roll(field, 1, field.ndim - 1))
    return up - down


def cross(p, q):
    return (p[1] * q[2] - p[2] * q[1], p[2] * q[0] - p[0] * q[2], p[0] * q[1] - p[1] * q[0])


def cross_first(p, q):
    return p[1] * q[2] - p[2] * q[1]


def coupled(curvature, grads):
    if curvature:
        dens, vel, dchange, vchange = grads
        mixed = tuple(s + t for s, t in zip(cross(dchange, vel), cross(dens, vchange)))
    else:
        dens, vel = grads
        mixed = cross(dens, vel)
    return dens, vel, mixed


def forces_kernel(
    grav_levels,
    grav_step,
    seis_levels,
    seis_step,
    labels_in,
    dens_index_in,
    vel_index_in,
    dens_table_in,
    vel_table_in,
    dens_out,
    vel_out,
    grav_slope,
    seis_slope,
    labels,
    dens_index,
    vel_index,
    dens_table,
    vel_table,
    gl,
    gs,
    sl,
    st,
    sb,
    hb,
    rb,
    db,
    xs,
    xr,
    q1e,
    q1s,
    q2s,
    acc,
    df,
    rs,
    rv,
    load_sem,
    leg1_send,
    leg1_recv,
    leg2_send,
    leg2_recv,
    xh_send,
    xh_recv,
    yd_send,
    yd_recv,
    yv_send,
    yv_recv,
    ret_send,
    ret_recv,
):
    me = Place()
    slab_rows = seis_levels.shape[1]

    loads = []
    for number, (source, target) in enumerate(
        [
            (labels_in, labels),
            (dens_index_in, dens_index),
            (vel_index_in, vel_index),
            (dens_table_in, dens_table),
            (vel_table_in, vel_table),
            (seis_levels, sl.at[:, pl.ds(PAD, slab_rows), :]),
            (seis_step, st.at[:, pl.ds(PAD, slab_rows), :]),
            (grav_levels, gl),
            (grav_step, gs),
        ]
    ):
        copy = pltpu.make_async_copy(source, target, load_sem.at[number])
        copy.start()
        loads.append(copy)

    barrier = pltpu.get_barrier_semaphore()

    def greet(device):
        pl.semaphore_signal(barrier, inc=1, device_id=device, device_id_type=MESH)

    def greet_first(i, _):
        device = me.first_leg(i // 2, i % 2, 0)[1]

        @pl.when(jnp.logical_not(me.is_me(device)))
        def _():
            greet(device)

        return 0

    lax.fori_loop(0, 8, greet_first, 0)

    def greet_second(i, _):
        y2, c2, far = i // 4, (i // 2) % 2, i % 2
        xr_mid = 1 + me.xl
        xr_end = 3 * me.xh
        x2 = far * xr_end + (1 - far) * xr_mid
        device = me.device(me.z, x2 // 2, c2, y2, x2 % 2)

        @pl.when(jnp.logical_not(me.is_me(device)))
        def _():
            greet(device)

        return 0

    lax.fori_loop(0, 16, greet_second, 0)

    def greet_return(i, _):
        device = (i, me.z * 2 + me.xh)

        @pl.when(jnp.logical_not(me.is_me(device)))
        def _():
            greet(device)

        return 0

    lax.fori_loop(0, 16, greet_return, 0)
    has_low_x, has_high_x = me.w > 0, me.w < 15
    has_low_y, has_high_y = me.n > 0, me.n < 7
    low_x, high_x = (me.w - 1, me.n), (me.w + 1, me.n)
    low_y, high_y = (me.w, me.n - 1), (me.w, me.n + 1)
    sides = ((has_low_x, low_x), (has_high_x, high_x), (has_low_y, low_y), (has_high_y, high_y))
    for here, device in sides:

        @pl.when(here)
        def _():
            greet(device)

    def not_me(device):
        return 1 - me.is_me(device).astype(jnp.int32)

    expected = 0
    for here, _ in sides:
        expected = expected + here.astype(jnp.int32)
    for i in range(8):
        expected = expected + not_me(me.first_leg(i // 2, i % 2, 0)[1])
    for i in range(16):
        expected = expected + not_me(me.second_leg(i // 4, (i // 2) % 2, i % 2)[1])
        expected = expected + not_me(me.slab(i))

    for copy in loads[:5]:
        copy.wait()
    dens_coeff = [0.5 * v for v in coeffs(labels, dens_index, dens_table)]
    vel_coeff = [0.5 * v for v in coeffs(labels, vel_index, vel_table)]

    def remote(source, target, send, recv, device):
        return pltpu.make_async_remote_copy(
            src_ref=source,
            dst_ref=target,
            send_sem=send,
            recv_sem=recv,
            device_id=device,
            device_id_type=MESH,
        )

    def start_any(source, target, send, recv, device):
        mine = me.is_me(device)

        @pl.when(mine)
        def _():
            pltpu.make_async_copy(source, target, recv).start()

        @pl.when(jnp.logical_not(mine))
        def _():
            remote(source, target, send, recv, device).start()

    def await_send(source, send, device):
        @pl.when(jnp.logical_not(me.is_me(device)))
        def _():
            remote(source, source, send, send, device).wait_send()

    def await_recv(target, recv):
        pltpu.make_async_copy(target, target, recv).wait()

    def message(field, slot):
        return sb.at[field, slot]

    def brick_slot(field, slot):
        return rb.at[field, pl.ds(pl.multiple_of((slot + 1) * MSG, 8), MSG), :]

    def route(i):
        dz, a, c2 = i // 4, (i // 2) % 2, i % 2
        return dz, a, c2

    def leg_two(field, i, source, finish=False):
        dz, a, c2 = route(i)
        slot, brick, there = me.second_leg(dz, a, c2)
        if finish:
            await_send(source, leg2_send.at[field, slot], brick)
        else:
            start_any(
                source,
                brick_slot(field, there),
                leg2_send.at[field, slot],
                leg2_recv.at[field, there],
                brick,
            )

    def send_slabs(field):
        def one(i, _):
            dz, a, c2 = route(i)
            block, relay, slot, stays = me.first_leg(dz, a, c2)
            x_at = block * NX - 2 + lax.broadcasted_iota(jnp.int32, (PITCH, 128), 0)
            inside = both(x_at >= 0, x_at < slab_rows // 2)
            for column in range(2):
                rows = pl.ds(block * 2 * NX + PAD - 4 + column, PITCH, stride=2)
                total = None
                for level in range(4):
                    t = jnp.tanh(sl[level, rows, :])
                    if field == 0:
                        term = vel_coeff[level] * (1.0 + t)
                    else:
                        term = (vel_coeff[level] * (1.0 - t * t)) * st[level, rows, :]
                    total = term if total is None else total + term
                sb[field, block, pl.ds(column * PITCH, PITCH), :] = jnp.where(inside, total, 0.0)

            @pl.when(stays)
            def _():
                leg_two(field, i, message(field, block))

            @pl.when(jnp.logical_not(stays))
            def _():
                remote(
                    message(field, block),
                    hb.at[field, slot],
                    leg1_send.at[field, block],
                    leg1_recv.at[field, slot],
                    relay,
                ).start()

            return 0

        lax.fori_loop(0, 16, one, 0)

    def relay_slabs(field):
        def one(i, _):
            dz, a, c2 = route(i)
            stays = me.first_leg(dz, a, c2)[3]
            slot = me.second_leg(dz, a, c2)[0]

            @pl.when(jnp.logical_not(stays))
            def _():
                await_recv(hb.at[field, slot], leg1_recv.at[field, slot])
                leg_two(field, i, hb.at[field, slot])

            return 0

        lax.fori_loop(0, 16, one, 0)

    loads[5].wait()
    pl.semaphore_wait(barrier, expected)
    send_slabs(0)
    loads[6].wait()
    send_slabs(1)

    loads[7].wait()
    loads[8].wait()

    def dens_row(x):
        dens, change = None, None
        for level in range(4):
            t = jnp.tanh(gl[level, x])
            term = dens_coeff[level] * (1.0 + t)
            slope = dens_coeff[level] * (1.0 - t * t)
            grav_slope[level, x] = slope * (1.0 / 16.0)
            slope = slope * gs[level, x]
            dens = term if dens is None else dens + term
            change = slope if change is None else change + slope
        rows = pl.ds(2 * PITCH + 2 + x, NY, stride=PITCH)
        db[0, rows, :] = dens
        db[1, rows, :] = change
        return dens, change

    def edge_row(k, _):
        side, row = k // 2, k % 2
        dens, change = dens_row(side * (NX - 2) + row)
        xs[side, pl.ds(pl.multiple_of(row * NY, 8), NY), :] = dens
        xs[side, pl.ds(pl.multiple_of((2 + row) * NY, 8), NY), :] = change
        return 0

    lax.fori_loop(0, 4, edge_row, 0)

    def x_halo(side):
        return remote(
            xs.at[side],
            xr.at[1 - side],
            xh_send.at[side],
            xh_recv.at[1 - side],
            (low_x, high_x)[side],
        )

    for side in range(2):

        @pl.when(sides[side][0])
        def _():
            x_halo(side).start()

    def inner_row(x, _):
        dens_row(x)
        return 0

    lax.fori_loop(2, NX - 2, inner_row, 0)

    relay_slabs(0)

    for side in range(2):
        rows = pl.ds(0, 2 * NY * 2)

        @pl.when(sides[side][0])
        def _():
            await_recv(xr.at[side], xh_recv.at[side])

        @pl.when(jnp.logical_not(sides[side][0]))
        def _():
            xr[side] = jnp.zeros(xr.shape[1:], jnp.float32)

        for field in range(2):
            for row in range(2):
                db[field, pl.ds(2 * PITCH + side * (NX + 2) + row, NY, stride=PITCH), :] = xr[
                    side, pl.ds((field * 2 + row) * NY, NY), :
                ]

    def y_halo(ref, send, recv, field, side):
        source = ref.at[field, pl.ds((2 + side * (NY - 2)) * PITCH, MSG), :]
        target = ref.at[field, pl.ds((1 - side) * (NY + 2) * PITCH, MSG), :]
        return remote(
            source, target, send.at[field, side], recv.at[field, 1 - side], (low_y, high_y)[side]
        )

    def y_halo_start(ref, send, recv, field):
        for side in range(2):

            @pl.when(sides[2 + side][0])
            def _():
                y_halo(ref, send, recv, field, side).start()

            @pl.when(jnp.logical_not(sides[2 + side][0]))
            def _():
                ref[field, pl.ds(side * (NY + 2) * PITCH, MSG), :] = jnp.zeros(
                    (MSG, 128), jnp.float32
                )

    def y_halo_recv(ref, send, recv, field):
        for side in range(2):

            @pl.when(sides[2 + side][0])
            def _():
                await_recv(
                    ref.at[field, pl.ds(side * (NY + 2) * PITCH, MSG), :], recv.at[field, side]
                )

    def y_halo_sent(ref, send, recv, field):
        for side in range(2):

            @pl.when(sides[2 + side][0])
            def _():
                y_halo(ref, send, recv, field, side).wait_send()

    for field in range(2):
        y_halo_start(db, yd_send, yd_recv, field)

    relay_slabs(1)

    def arrive(field):
        for slot in (0, 15):
            await_recv(brick_slot(field, slot), leg2_recv.at[field, slot])
        y_halo_start(rb, yv_send, yv_recv, field)

        def one(slot, _):
            await_recv(brick_slot(field, slot), leg2_recv.at[field, slot])
            return 0

        lax.fori_loop(1, 15, one, 0)

    arrive(0)
    for field in range(2):
        y_halo_recv(db, yd_send, yd_recv, field)
    y_halo_recv(rb, yv_send, yv_recv, 0)

    def gradient(ref, field, yy):
        def at(column, x):
            return ref[field, pl.ds(column * PITCH + 2 + x, NX), :]

        return (
            at(yy, 1) - at(yy, -1),
            at(yy + 1, 0) - at(yy - 1, 0),
            depth_change(at(yy, 0)),
        )

    def edge_gradient(ref, field, x):
        def at(dy, x):
            return ref[field, pl.ds((2 + dy) * PITCH + 2 + x, NY, stride=PITCH), :]

        return (at(0, x + 1) - at(0, x - 1), at(1, x) - at(-1, x), depth_change(at(0, x)))

    def compute(field):
        which = [(db, 0), (rb, 0), (db, 1), (rb, 1)][: 2 + 2 * field]

        for side in range(2):
            x = (-1, NX)[side]
            dens, vel, mixed = coupled(field, [edge_gradient(r, f, x) for r, f in which])
            keep = sides[side][0].astype(jnp.float32)
            q1e[0, side] = cross_first(vel, mixed) * keep
            q1e[1, side] = cross_first(mixed, dens) * keep

        def column(yy):
            dens, vel, mixed = coupled(field, [gradient(r, f, yy) for r, f in which])
            outside = jnp.logical_or(
                both(yy == 1, me.n == 0), both(yy == NY + 2, me.n == 7)
            )
            keep = 1.0 - outside.astype(jnp.float32)
            y = jnp.clip(yy - 2, 0, NY - 1)
            for out, q in enumerate((cross(vel, mixed), cross(mixed, dens))):
                q1s[out, pl.ds(8, NX), :] = q[0]
                q1s[out, pl.ds(7, 1), :] = q1e[out, 0, pl.ds(y, 1), :]
                q1s[out, pl.ds(8 + NX, 1), :] = q1e[out, 1, pl.ds(y, 1), :]
                along_x = q1s[out, pl.ds(7, NX), :] - q1s[out, pl.ds(9, NX), :]
                q2s[out, yy] = q[1] * keep
                acc[out, yy] = along_x - depth_change(q[2])

        column(1)
        column(2)

        def pair(p, _):
            for half in range(2):
                yy = 2 * p + 2 + half
                column(yy + 1)
                df[field, pl.ds(pl.multiple_of((yy - 2) * NX, 8), NX), :] = acc[0, yy] + (
                    q2s[0, yy - 1] - q2s[0, yy + 1]
                )
                rs[field, p, pl.ds(half * NX, NX), :] = acc[1, yy] + (
                    q2s[1, yy - 1] - q2s[1, yy + 1]
                )
            start_any(
                rs.at[field, p],
                rv.at[field, me.w],
                ret_send.at[field, p],
                ret_recv.at[field, me.w],
                me.slab(p),
            )
            return 0

        lax.fori_loop(0, 16, pair, 0)

    compute(0)
    arrive(1)
    y_halo_recv(rb, yv_send, yv_recv, 1)
    compute(1)

    for field in range(2):

        def turn(x, _):
            dens_out[field, x] = df[field, pl.ds(x, NY, stride=NX), :]
            return 0

        lax.fori_loop(0, NX, turn, 0)

    def seis_rows(i, _):
        for level in range(4):
            t = jnp.tanh(sl[level, pl.ds(pl.multiple_of(PAD + i * 32, 8), 32), :])
            scale = vel_coeff[level] * (1.0 / 16.0)
            seis_slope[level, pl.ds(pl.multiple_of(i * 32, 8), 32), :] = scale * (1.0 - t * t)
        return 0

    lax.fori_loop(0, slab_rows // 32, seis_rows, 0)

    for field in range(2):

        def finish(block, _):
            await_recv(rv.at[field, block], ret_recv.at[field, block])
            for half in range(2):
                vel_out[field, pl.ds(block * 2 * NX + half, NX, stride=2), :] = rv[
                    field, block, pl.ds(half * NX, NX), :
                ]
            return 0

        lax.fori_loop(0, 16, finish, 0)

    for side in range(2):

        @pl.when(sides[side][0])
        def _():
            x_halo(side).wait_send()

    for field in range(2):
        y_halo_sent(db, yd_send, yd_recv, field)
        y_halo_sent(rb, yv_send, yv_recv, field)

        def sent(i, _):
            dz, a, c2 = route(i)
            block, relay, slot, stays = me.first_leg(dz, a, c2)

            @pl.when(jnp.logical_not(stays))
            def _():
                remote(
                    message(field, block),
                    message(field, block),
                    leg1_send.at[field, block],
                    leg1_send.at[field, block],
                    relay,
                ).wait_send()

            leg_two(field, i, hb.at[field, 0], finish=True)
            await_send(rs.at[field, 0], ret_send.at[field, i], me.slab(i))
            return 0

        lax.fori_loop(0, 16, sent, 0)


def chain_kernel(
    steps,
    dens_force,
    vel_force,
    grav_slope,
    seis_slope,
    grav_gradient,
    grav_curvature,
    seis_gradient,
    seis_curvature,
):
    for slope, force, outs in (
        (grav_slope, dens_force, (grav_gradient, grav_curvature)),
        (seis_slope, vel_force, (seis_gradient, seis_curvature)),
    ):
        rows = slope.shape[1] // steps
        here = pl.ds(pl.program_id(0) * rows, rows)
        for level in range(4):
            factor = slope[level, here]
            for number in range(2):
                outs[number][level] = factor * force[number, here]


def shards(
    grav_levels,
    grav_step,
    seis_levels,
    seis_step,
    unit_labels,
    dens_index,
    vel_index,
    dens_table,
    vel_table,
):
    levels, nx, ny, nz = grav_levels.shape
    slab_x, slab_y = seis_levels.shape[1:3]
    rows = slab_x * slab_y
    seis_rows = seis_levels.reshape(levels, rows, nz)
    step_rows = seis_step.reshape(levels, rows, nz)
    tables = (unit_labels, dens_index, vel_index, dens_table, vel_table)
    hbm = pl.BlockSpec(memory_space=pltpu.HBM)
    vmem = pl.BlockSpec(memory_space=pltpu.VMEM)
    f32 = jnp.float32
    dma = pltpu.SemaphoreType.DMA
    brick_shape = jax.ShapeDtypeStruct(grav_levels.shape, f32)
    slab_shape = jax.ShapeDtypeStruct(seis_rows.shape, f32)
    forces = pl.pallas_call(
        forces_kernel,
        out_shape=(
            jax.ShapeDtypeStruct((2, nx, ny, nz), f32),
            jax.ShapeDtypeStruct((2, rows, nz), f32),
            brick_shape,
            slab_shape,
        ),
        in_specs=[hbm] * 9,
        out_specs=(vmem,) * 4,
        scratch_shapes=[
            *(pltpu.SMEM(table.shape, table.dtype) for table in tables),
            pltpu.VMEM((levels, nx, ny, nz), f32),
            pltpu.VMEM((levels, nx, ny, nz), f32),
            pltpu.VMEM((levels, rows + 4 * PAD, nz), f32),
            pltpu.VMEM((levels, rows + 4 * PAD, nz), f32),
            pltpu.VMEM((2, 16, MSG, nz), f32),
            pltpu.VMEM((2, 16, MSG, nz), f32),
            pltpu.VMEM((2, COLS, nz), f32),
            pltpu.VMEM((2, COLS, nz), f32),
            pltpu.VMEM((2, 4 * NY, nz), f32),
            pltpu.VMEM((2, 4 * NY, nz), f32),
            pltpu.VMEM((2, 2, NY, nz), f32),
            pltpu.VMEM((2, NX + 16, nz), f32),
            pltpu.VMEM((2, NY + 4, NX, nz), f32),
            pltpu.VMEM((2, NY + 4, NX, nz), f32),
            pltpu.VMEM((2, NY * NX, nz), f32),
            pltpu.VMEM((2, 16, 2 * NX, nz), f32),
            pltpu.VMEM((2, 16, 2 * NX, nz), f32),
            dma((9,)),
            dma((2, 16)),
            dma((2, 16)),
            dma((2, 16)),
            dma((2, 16)),
            dma((2,)),
            dma((2,)),
            dma((2, 2)),
            dma((2, 2)),
            dma((2, 2)),
            dma((2, 2)),
            dma((2, 16)),
            dma((2, 16)),
        ],
        compiler_params=pltpu.CompilerParams(
            collective_id=0, has_side_effects=True, vmem_limit_bytes=40 << 20
        ),
        name="forces",
    )(*(pltpu.with_memory_space_constraint(v, pltpu.HBM) for v in (grav_levels, grav_step, seis_rows, step_rows, *tables)))

    steps = 8
    brick = pl.BlockSpec((levels, nx // steps, ny, nz), lambda i: (0, i, 0, 0))
    slab = pl.BlockSpec((levels, rows // steps, nz), lambda i: (0, i, 0))
    outs = pl.pallas_call(
        functools.partial(chain_kernel, steps),
        grid=(steps,),
        out_shape=(brick_shape, brick_shape, slab_shape, slab_shape),
        in_specs=[vmem] * 4,
        out_specs=(brick, brick, slab, slab),
        compiler_params=pltpu.CompilerParams(vmem_limit_bytes=32 << 20),
        name="chain",
    )(*forces)
    return (
        outs[0],
        outs[1],
        outs[2].reshape(seis_levels.shape),
        outs[3].reshape(seis_levels.shape),
    )


def solution(mesh):
    placed = (
        P(None, "wide", "narrow", None),
        P(None, "wide", "narrow", None),
        P(None, None, ("wide", "narrow"), None),
        P(None, None, ("wide", "narrow"), None),
        P(),
        P(),
        P(),
        P(),
        P(),
    )
    return jax.shard_map(
        shards,
        mesh=mesh,
        in_specs=placed,
        out_specs=placed[:4],
        check_vma=False,
    )
```

```python
import functools

import jax
import jax.numpy as jnp
from jax import lax
from jax.experimental import pallas as pl
from jax.experimental.pallas import tpu as pltpu
from jax.sharding import PartitionSpec as P

MESH = pl.DeviceIdType.MESH
NX = 32
NY = 32
PITCH = NX + 4
MSG = 2 * PITCH
COLS = (NY + 4) * PITCH
PAD = 8


def both(one, other):
    return jnp.logical_and(one, other)


class Place:
    def __init__(self):
        self.w = lax.axis_index("wide")
        self.n = lax.axis_index("narrow")
        self.z = self.w // 4
        self.xh = (self.w // 2) % 2
        self.c = self.w % 2
        self.y = self.n // 2
        self.xl = self.n % 2
        self.x = self.xh * 2 + self.xl
        self.mid = (self.xh + self.xl) % 2

    @staticmethod
    def device(z, xh, c, y, xl):
        return (z * 4 + xh * 2 + c, y * 2 + xl)

    def is_me(self, device):
        return both(device[0] == self.w, device[1] == self.n)

    def across(self, a):
        return self.x + (1 - self.mid) * a * (3 - 2 * self.x)

    def step(self, i):
        pair, half = i // 2, i % 2
        return pair // 2 + 2 * half, (pair + half) % 2

    def side(self, e):
        return 1 - e + (1 - self.xh) * self.xl * (2 * e - 1)

    def first_leg(self, i):
        d, e = self.step(i)
        a = self.side(e)
        z2 = (self.z + self.y + d) % 4
        xr = self.across(a)
        xh2 = self.mid * a + (1 - self.mid) * (xr // 2)
        return z2 * 2 + xh2, self.device(z2, xr // 2, self.c, self.y, xr % 2)

    def second_leg(self, i, c2):
        d, e = self.step(i)
        a = self.side(e)
        zs = (self.z + 8 - self.y - d) % 4
        xs = self.across(a)
        xh2 = self.mid * a + (1 - self.mid) * self.xh
        brick = self.device(self.z, xh2, c2, zs, xs // 2)
        return brick, self.c * 8 + self.y * 2 + xs % 2

    def way_back(self, i, c2):
        d, e = self.step(i)
        y2 = (self.y + self.z + d) % 4
        pair = c2 * 8 + y2 * 2 + (self.xh + e) % 2
        return pair, (self.n * 2 + c2, pair % 8)


def coeffs(labels, index, table):
    return [table[index[labels[level]]] for level in range(4)]


def depth_change(field):
    lane = lax.broadcasted_iota(jnp.int32, field.shape, field.ndim - 1)
    up = jnp.where(lane == 127, 0.0, pltpu.roll(field, 127, field.ndim - 1))
    down = jnp.where(lane == 0, 0.0, pltpu.roll(field, 1, field.ndim - 1))
    return up - down


def cross(p, q):
    return (p[1] * q[2] - p[2] * q[1], p[2] * q[0] - p[0] * q[2], p[0] * q[1] - p[1] * q[0])


def forces_kernel(
    grav_levels,
    grav_step,
    seis_levels,
    seis_step,
    labels_in,
    dens_index_in,
    vel_index_in,
    dens_table_in,
    vel_table_in,
    dens_out,
    vel_out,
    grav_slope,
    seis_slope,
    labels,
    dens_index,
    vel_index,
    dens_table,
    vel_table,
    gl,
    gs,
    sl,
    st,
    sb,
    hb,
    rb,
    db,
    xs,
    xr,
    grads,
    edge_grads,
    mixes,
    edge_mixes,
    q1e,
    q1s,
    q2s,
    acc,
    df,
    rs,
    rv,
    load_sem,
    leg1_send,
    leg1_recv,
    leg2_send,
    leg2_recv,
    xh_send,
    xh_recv,
    yd_send,
    yd_recv,
    yv_send,
    yv_recv,
    ret_send,
    ret_recv,
):
    me = Place()
    slab_rows = seis_levels.shape[1]

    loads = []
    for number, (source, target) in enumerate(
        [
            (labels_in, labels),
            (dens_index_in, dens_index),
            (vel_index_in, vel_index),
            (dens_table_in, dens_table),
            (vel_table_in, vel_table),
            (seis_levels, sl.at[:, pl.ds(PAD, slab_rows), :]),
            (seis_step, st.at[:, pl.ds(PAD, slab_rows), :]),
            (grav_levels, gl),
            (grav_step, gs),
        ]
    ):
        copy = pltpu.make_async_copy(source, target, load_sem.at[number])
        copy.start()
        loads.append(copy)

    barrier = pltpu.get_barrier_semaphore()

    def greet(device):
        pl.semaphore_signal(barrier, inc=1, device_id=device, device_id_type=MESH)

    for dz in range(1, 4):
        greet(me.device((me.z + dz) % 4, me.xh, me.c, me.y, me.xl))

    @pl.when(me.mid == 0)
    def _():
        for z2 in range(4):
            greet(me.device(z2, 1 - me.xh, me.c, me.y, 1 - me.xl))

    for far in range(2):
        x2 = 3 * me.xh if far else 1 + me.xl
        for y2 in range(4):
            for c2 in range(2):
                device = me.device(me.z, x2 // 2, c2, y2, x2 % 2)
                if far:

                    @pl.when(jnp.logical_not(me.is_me(device)))
                    def _():
                        greet(device)

                else:
                    greet(device)

    has_low_x, has_high_x = me.w > 0, me.w < 15
    has_low_y, has_high_y = me.n > 0, me.n < 7
    low_x, high_x = (me.w - 1, me.n), (me.w + 1, me.n)
    low_y, high_y = (me.w, me.n - 1), (me.w, me.n + 1)
    sides = ((has_low_x, low_x), (has_high_x, high_x), (has_low_y, low_y), (has_high_y, high_y))
    for here, device in sides:

        @pl.when(here)
        def _():
            greet(device)

    expected = 3 + 4 * (1 - me.mid) + 15 + me.mid
    for here, _ in sides:
        expected = expected + here.astype(jnp.int32)

    for copy in loads[:5]:
        copy.wait()
    dens_coeff = [0.5 * v for v in coeffs(labels, dens_index, dens_table)]
    vel_coeff = [0.5 * v for v in coeffs(labels, vel_index, vel_table)]

    def remote(source, target, send, recv, device):
        return pltpu.make_async_remote_copy(
            src_ref=source,
            dst_ref=target,
            send_sem=send,
            recv_sem=recv,
            device_id=device,
            device_id_type=MESH,
        )

    def start_any(source, target, send, recv, device):
        mine = me.is_me(device)

        @pl.when(mine)
        def _():
            pltpu.make_async_copy(source, target, recv).start()

        @pl.when(jnp.logical_not(mine))
        def _():
            remote(source, target, send, recv, device).start()

    def await_bytes(ref, sem):
        pltpu.make_async_copy(ref, ref, sem).wait()

    def brick_slot(field, slot):
        return rb.at[field, pl.ds(pl.multiple_of((slot + 1) * MSG, 8), MSG), :]

    def send_slabs(field):
        def one(i, _):
            send_slab(field, i)
            return 0

        lax.fori_loop(0, 8, one, 0)

    def send_slab(field, i):
        pair, relay = me.first_leg(i)
        for c2 in range(2):
            block = pair * 2 + c2
            x_at = block * NX - 2 + lax.broadcasted_iota(jnp.int32, (PITCH, 128), 0)
            inside = both(x_at >= 0, x_at < slab_rows // 2)
            for column in range(2):
                rows = pl.ds(block * 2 * NX + PAD - 4 + column, PITCH, stride=2)
                total = None
                for level in range(4):
                    t = jnp.tanh(sl[level, rows, :])
                    if field == 0:
                        term = vel_coeff[level] * (1.0 + t)
                    else:
                        term = (vel_coeff[level] * (1.0 - t * t)) * st[level, rows, :]
                    total = term if total is None else total + term
                sb[field, i, pl.ds((c2 * 2 + column) * PITCH, PITCH), :] = jnp.where(
                    inside, total, 0.0
                )
        start_any(
            sb.at[field, i], hb.at[field, i], leg1_send.at[field], leg1_recv.at[field, i], relay
        )

    def relay_slab(field, i):
        await_bytes(hb.at[field, i], leg1_recv.at[field, i])
        for c2 in range(2):
            brick, slot = me.second_leg(i, c2)
            which = (slot > 0).astype(jnp.int32) + (slot > 14).astype(jnp.int32)
            start_any(
                hb.at[field, i, pl.ds(c2 * MSG, MSG), :],
                brick_slot(field, slot),
                leg2_send.at[field],
                leg2_recv.at[field, which],
                brick,
            )

    loads[5].wait()
    pl.semaphore_wait(barrier, expected)
    send_slabs(0)

    loads[7].wait()
    loads[8].wait()

    def dens_row(x):
        dens, change = None, None
        for level in range(4):
            t = jnp.tanh(gl[level, x])
            term = dens_coeff[level] * (1.0 + t)
            slope = dens_coeff[level] * (1.0 - t * t)
            grav_slope[level, x] = slope * (1.0 / 16.0)
            slope = slope * gs[level, x]
            dens = term if dens is None else dens + term
            change = slope if change is None else change + slope
        rows = pl.ds(2 * PITCH + 2 + x, NY, stride=PITCH)
        db[0, rows, :] = dens
        db[1, rows, :] = change
        return dens, change

    def edge_row(k, _):
        side, row = k // 2, k % 2
        dens, change = dens_row(side * (NX - 2) + row)
        xs[side, pl.ds(pl.multiple_of(row * NY, 8), NY), :] = dens
        xs[side, pl.ds(pl.multiple_of((2 + row) * NY, 8), NY), :] = change
        return 0

    lax.fori_loop(0, 4, edge_row, 0)

    def x_halo(side):
        return remote(
            xs.at[side],
            xr.at[1 - side],
            xh_send.at[side],
            xh_recv.at[1 - side],
            (low_x, high_x)[side],
        )

    for side in range(2):

        @pl.when(sides[side][0])
        def _():
            x_halo(side).start()

    def inner_row(x, _):
        dens_row(x)
        return 0

    lax.fori_loop(2, NX - 2, inner_row, 0)

    loads[6].wait()

    def relay_and_send(i, _):
        relay_slab(0, i)
        send_slab(1, i)
        return 0

    lax.fori_loop(0, 8, relay_and_send, 0)

    for side in range(2):
        rows = pl.ds(0, 2 * NY * 2)

        @pl.when(sides[side][0])
        def _():
            await_bytes(xr.at[side], xh_recv.at[side])

        @pl.when(jnp.logical_not(sides[side][0]))
        def _():
            xr[side] = jnp.zeros(xr.shape[1:], jnp.float32)

        for field in range(2):
            for row in range(2):
                db[field, pl.ds(2 * PITCH + side * (NX + 2) + row, NY, stride=PITCH), :] = xr[
                    side, pl.ds((field * 2 + row) * NY, NY), :
                ]

    def y_halo(ref, send, recv, field, side):
        source = ref.at[field, pl.ds((2 + side * (NY - 2)) * PITCH, MSG), :]
        target = ref.at[field, pl.ds((1 - side) * (NY + 2) * PITCH, MSG), :]
        return remote(
            source, target, send.at[field, side], recv.at[field, 1 - side], (low_y, high_y)[side]
        )

    def y_halo_start(ref, send, recv, field):
        for side in range(2):

            @pl.when(sides[2 + side][0])
            def _():
                y_halo(ref, send, recv, field, side).start()

            @pl.when(jnp.logical_not(sides[2 + side][0]))
            def _():
                ref[field, pl.ds(side * (NY + 2) * PITCH, MSG), :] = jnp.zeros(
                    (MSG, 128), jnp.float32
                )

    def y_halo_recv(ref, send, recv, field):
        for side in range(2):

            @pl.when(sides[2 + side][0])
            def _():
                await_bytes(
                    ref.at[field, pl.ds(side * (NY + 2) * PITCH, MSG), :], recv.at[field, side]
                )

    def y_halo_sent(ref, send, recv, field):
        for side in range(2):

            @pl.when(sides[2 + side][0])
            def _():
                y_halo(ref, send, recv, field, side).wait_send()

    for field in range(2):
        y_halo_start(db, yd_send, yd_recv, field)

    def relay_second(i, _):
        relay_slab(1, i)
        return 0

    def gradient(ref, field, yy):
        def at(column, x):
            return ref[field, pl.ds(column * PITCH + 2 + x, NX), :]

        return (
            at(yy, 1) - at(yy, -1),
            at(yy + 1, 0) - at(yy - 1, 0),
            depth_change(at(yy, 0)),
        )

    def edge_gradient(ref, field, side, rows):
        x = (-1, NX)[side]

        def at(dy, x):
            start = (rows.start + 2 + dy) * PITCH + 2 + x
            return ref[field, pl.ds(start, rows.size, stride=PITCH), :]

        return (at(0, x + 1) - at(0, x - 1), at(1, x) - at(-1, x), depth_change(at(0, x)))

    every, inner_rows = pl.ds(0, NY), pl.ds(1, NY - 2)

    def keep(ref, *at_and_vector):
        *at, vector = at_and_vector
        for number in range(3):
            ref[(at[0], number, *at[1:])] = vector[number]

    def kept(ref, *at):
        return tuple(ref[(at[0], number, *at[1:])] for number in range(3))

    def columns(body, first, count, batch):
        def some(j, _):
            body([first + j * batch + k for k in range(batch)])
            return 0

        lax.fori_loop(0, count // batch, some, 0)

    def dens_gradient(field):
        def some(yys):
            for yy in yys:
                keep(grads, field, yy, gradient(db, field, yy))

        columns(some, 2, NY, 4)
        some([1, NY + 2])
        for side in range(2):
            keep(edge_grads, field, side, every, edge_gradient(db, field, side, every))

    def mixed(field, own, grads, *at):
        first = cross(kept(grads, 0, *at), own)
        if field == 0:
            return first
        second = cross(kept(grads, 1, *at), kept(grads, 2, *at))
        return tuple(s + t for s, t in zip(second, first))

    def masked(vector, inside):
        factor = inside.astype(jnp.float32)
        return tuple(v * factor for v in vector)

    def vel_columns(field, yys, inside=None):
        qs = []
        for number, yy in enumerate(yys):
            own = gradient(rb, field, yy)
            mix = mixed(field, own, grads, yy)
            if inside is not None:
                mix = masked(mix, inside[number])
            keep(grads, 2 + field, yy, own)
            keep(mixes, field, yy, mix)
            qs.append(cross(mix, kept(grads, 0, yy)))
        collect(qs, yys)

    def vel_edges(field, rows):
        for side in range(2):
            own = edge_gradient(rb, field, side, rows)
            mix = masked(mixed(field, own, edge_grads, side, rows), sides[side][0])
            keep(edge_grads, 2 + field, side, rows, own)
            keep(edge_mixes, field, side, rows, mix)
            dens = kept(edge_grads, 0, side, rows)
            q1e[side, rows] = mix[1] * dens[2] - mix[2] * dens[1]

    def dens_columns(field, yys):
        collect([cross(kept(grads, 2, yy), kept(mixes, field, yy)) for yy in yys], yys)

    def dens_edges(field):
        for side in range(2):
            vel, mix = kept(edge_grads, 2, side, every), kept(edge_mixes, field, side, every)
            q1e[side] = vel[1] * mix[2] - vel[2] * mix[1]

    def collect(qs, yys):
        for k, (q, yy) in enumerate(zip(qs, yys)):
            y = jnp.clip(yy - 2, 0, NY - 1)
            q1s[k, pl.ds(8, NX), :] = q[0]
            q1s[k, pl.ds(7, 1), :] = q1e[0, pl.ds(y, 1), :]
            q1s[k, pl.ds(8 + NX, 1), :] = q1e[1, pl.ds(y, 1), :]
            q2s[yy] = q[1]
        turned = [depth_change(q[2]) for q in qs]
        for k, yy in enumerate(yys):
            acc[yy] = q1s[k, pl.ds(7, NX), :] - q1s[k, pl.ds(9, NX), :] - turned[k]

    def adjoint(yy):
        return acc[yy] + (q2s[yy - 1] - q2s[yy + 1])

    def compute(field):
        vel_edges(field, inner_rows)

        columns(lambda yys: vel_columns(field, yys), 3, NY - 2, 5)
        y_halo_recv(rb, yv_send, yv_recv, field)
        vel_edges(field, every)
        true = me.n >= 0
        vel_columns(field, [1, 2, NY + 1, NY + 2], [me.n > 0, true, true, me.n < 7])

        def back(i, _):
            for c2 in range(2):
                p, slab = me.way_back(i, c2)
                for half in range(2):
                    rs[field, p, pl.ds(half * NX, NX), :] = adjoint(2 * p + 2 + half)
                start_any(
                    rs.at[field, p], rv.at[field, me.w], ret_send.at[field], ret_recv.at[field], slab
                )
            return 0

        lax.fori_loop(0, 8, back, 0)

    def arrive(field):
        for slot in (0, 15):
            await_bytes(brick_slot(field, slot), leg2_recv.at[field, slot // 15 * 2])
        y_halo_start(rb, yv_send, yv_recv, field)
        await_bytes(rb.at[field, pl.ds(2 * MSG, 14 * MSG), :], leg2_recv.at[field, 1])

    for field in range(2):
        y_halo_recv(db, yd_send, yd_recv, field)
        dens_gradient(field)
    lax.fori_loop(0, 8, relay_second, 0)
    arrive(0)
    compute(0)
    arrive(1)
    compute(1)

    for field in range(2):
        dens_edges(field)

        columns(lambda yys: dens_columns(field, yys), 2, NY, 4)
        dens_columns(field, [1, NY + 2])

        def keep_force(y, _):
            for k in range(4):
                at = pl.ds(pl.multiple_of((4 * y + k) * NX, 8), NX)
                df[field, at, :] = adjoint(4 * y + k + 2)
            return 0

        lax.fori_loop(0, NY // 4, keep_force, 0)

    for field in range(2):

        def turn(x, _):
            dens_out[field, x] = df[field, pl.ds(x, NY, stride=NX), :]
            return 0

        lax.fori_loop(0, NX, turn, 0)

    def seis_rows(i, _):
        for level in range(4):
            t = jnp.tanh(sl[level, pl.ds(pl.multiple_of(PAD + i * 32, 8), 32), :])
            scale = vel_coeff[level] * (1.0 / 16.0)
            seis_slope[level, pl.ds(pl.multiple_of(i * 32, 8), 32), :] = scale * (1.0 - t * t)
        return 0

    lax.fori_loop(0, slab_rows // 32, seis_rows, 0)

    for field in range(2):

        await_bytes(rv.at[field], ret_recv.at[field])

        def finish(block, _):
            for half in range(2):
                vel_out[field, pl.ds(block * 2 * NX + half, NX, stride=2), :] = rv[
                    field, block, pl.ds(half * NX, NX), :
                ]
            return 0

        lax.fori_loop(0, 16, finish, 0)

    for side in range(2):

        @pl.when(sides[side][0])
        def _():
            x_halo(side).wait_send()

    for field in range(2):
        y_halo_sent(db, yd_send, yd_recv, field)
        y_halo_sent(rb, yv_send, yv_recv, field)

        await_bytes(sb.at[field, pl.ds(0, 6)], leg1_send.at[field])
        await_bytes(rb.at[field, pl.ds(0, 15 * MSG), :], leg2_send.at[field])
        await_bytes(rs.at[field, pl.ds(0, 15)], ret_send.at[field])

        @pl.when(me.mid == 0)
        def _():
            await_bytes(sb.at[field, 0], leg1_send.at[field])

        @pl.when(me.mid == 1)
        def _():
            await_bytes(rb.at[field, pl.ds(0, MSG), :], leg2_send.at[field])

        @pl.when(me.w // 2 != me.n)
        def _():
            await_bytes(rs.at[field, 0], ret_send.at[field])


def chain_kernel(
    steps,
    dens_force,
    vel_force,
    grav_slope,
    seis_slope,
    grav_gradient,
    grav_curvature,
    seis_gradient,
    seis_curvature,
):
    for slope, force, outs in (
        (grav_slope, dens_force, (grav_gradient, grav_curvature)),
        (seis_slope, vel_force, (seis_gradient, seis_curvature)),
    ):
        rows = slope.shape[1] // steps
        here = pl.ds(pl.program_id(0) * rows, rows)
        for level in range(4):
            factor = slope[level, here]
            for number in range(2):
                outs[number][level] = factor * force[number, here]


def shards(
    grav_levels,
    grav_step,
    seis_levels,
    seis_step,
    unit_labels,
    dens_index,
    vel_index,
    dens_table,
    vel_table,
):
    levels, nx, ny, nz = grav_levels.shape
    slab_x, slab_y = seis_levels.shape[1:3]
    rows = slab_x * slab_y
    seis_rows = seis_levels.reshape(levels, rows, nz)
    step_rows = seis_step.reshape(levels, rows, nz)
    tables = (unit_labels, dens_index, vel_index, dens_table, vel_table)
    hbm = pl.BlockSpec(memory_space=pltpu.HBM)
    vmem = pl.BlockSpec(memory_space=pltpu.VMEM)
    f32 = jnp.float32
    dma = pltpu.SemaphoreType.DMA
    brick_shape = jax.ShapeDtypeStruct(grav_levels.shape, f32)
    slab_shape = jax.ShapeDtypeStruct(seis_rows.shape, f32)
    forces = pl.pallas_call(
        forces_kernel,
        out_shape=(
            jax.ShapeDtypeStruct((2, nx, ny, nz), f32),
            jax.ShapeDtypeStruct((2, rows, nz), f32),
            brick_shape,
            slab_shape,
        ),
        in_specs=[hbm] * 9,
        out_specs=(vmem,) * 4,
        scratch_shapes=[
            *(pltpu.SMEM(table.shape, table.dtype) for table in tables),
            pltpu.VMEM((levels, nx, ny, nz), f32),
            pltpu.VMEM((levels, nx, ny, nz), f32),
            pltpu.VMEM((levels, rows + 4 * PAD, nz), f32),
            pltpu.VMEM((levels, rows + 4 * PAD, nz), f32),
            pltpu.VMEM((2, 8, 2 * MSG, nz), f32),
            pltpu.VMEM((2, 8, 2 * MSG, nz), f32),
            pltpu.VMEM((2, COLS, nz), f32),
            pltpu.VMEM((2, COLS, nz), f32),
            pltpu.VMEM((2, 4 * NY, nz), f32),
            pltpu.VMEM((2, 4 * NY, nz), f32),
            pltpu.VMEM((4, 3, NY + 4, NX, nz), f32),
            pltpu.VMEM((4, 3, 2, NY, nz), f32),
            pltpu.VMEM((2, 3, NY + 4, NX, nz), f32),
            pltpu.VMEM((2, 3, 2, NY, nz), f32),
            pltpu.VMEM((2, NY, nz), f32),
            pltpu.VMEM((5, NX + 16, nz), f32),
            pltpu.VMEM((NY + 4, NX, nz), f32),
            pltpu.VMEM((NY + 4, NX, nz), f32),
            pltpu.VMEM((2, NY * NX, nz), f32),
            pltpu.VMEM((2, 16, 2 * NX, nz), f32),
            pltpu.VMEM((2, 16, 2 * NX, nz), f32),
            dma((9,)),
            dma((2,)),
            dma((2, 8)),
            dma((2,)),
            dma((2, 3)),
            dma((2,)),
            dma((2,)),
            dma((2, 2)),
            dma((2, 2)),
            dma((2, 2)),
            dma((2, 2)),
            dma((2,)),
            dma((2,)),
        ],
        compiler_params=pltpu.CompilerParams(
            collective_id=0, has_side_effects=True, vmem_limit_bytes=42 << 20
        ),
        name="forces",
    )(*(pltpu.with_memory_space_constraint(v, pltpu.HBM) for v in (grav_levels, grav_step, seis_rows, step_rows, *tables)))

    steps = 8
    brick = pl.BlockSpec((levels, nx // steps, ny, nz), lambda i: (0, i, 0, 0))
    slab = pl.BlockSpec((levels, rows // steps, nz), lambda i: (0, i, 0))
    outs = pl.pallas_call(
        functools.partial(chain_kernel, steps),
        grid=(steps,),
        out_shape=(brick_shape, brick_shape, slab_shape, slab_shape),
        in_specs=[vmem] * 4,
        out_specs=(brick, brick, slab, slab),
        compiler_params=pltpu.CompilerParams(vmem_limit_bytes=32 << 20),
        name="chain",
    )(*forces)
    return (
        outs[0],
        outs[1],
        outs[2].reshape(seis_levels.shape),
        outs[3].reshape(seis_levels.shape),
    )


def solution(mesh):
    placed = (
        P(None, "wide", "narrow", None),
        P(None, "wide", "narrow", None),
        P(None, None, ("wide", "narrow"), None),
        P(None, None, ("wide", "narrow"), None),
        P(),
        P(),
        P(),
        P(),
        P(),
    )
    return jax.shard_map(
        shards,
        mesh=mesh,
        in_specs=placed,
        out_specs=placed[:4],
        check_vma=False,
    )
```

```python
import functools

import jax
import jax.numpy as jnp
from jax import lax
from jax.experimental import pallas as pl
from jax.experimental.pallas import tpu as pltpu
from jax.sharding import PartitionSpec as P

MESH = pl.DeviceIdType.MESH
NX = 32
NY = 32
PITCH = NX + 4
MSG = 2 * PITCH
COLS = (NY + 4) * PITCH
PAD = 8


def both(one, other):
    return jnp.logical_and(one, other)


class Place:
    def __init__(self):
        self.w = lax.axis_index("wide")
        self.n = lax.axis_index("narrow")
        self.z = self.w // 4
        self.xh = (self.w // 2) % 2
        self.c = self.w % 2
        self.y = self.n // 2
        self.xl = self.n % 2
        self.x = self.xh * 2 + self.xl
        self.mid = (self.xh + self.xl) % 2

    @staticmethod
    def device(z, xh, c, y, xl):
        return (z * 4 + xh * 2 + c, y * 2 + xl)

    def is_me(self, device):
        return both(device[0] == self.w, device[1] == self.n)

    def across(self, a):
        return self.x + (1 - self.mid) * a * (3 - 2 * self.x)

    def step(self, i):
        pair, half = i // 2, i % 2
        return pair // 2 + 2 * half, (pair + half) % 2

    def side(self, e):
        return 1 - e + (1 - self.xh) * self.xl * (2 * e - 1)

    def first_leg(self, i):
        d, e = self.step(i)
        a = self.side(e)
        z2 = (self.z + self.y + d) % 4
        xr = self.across(a)
        xh2 = self.mid * a + (1 - self.mid) * (xr // 2)
        return z2 * 2 + xh2, self.device(z2, xr // 2, self.c, self.y, xr % 2)

    def second_leg(self, i, c2):
        d, e = self.step(i)
        a = self.side(e)
        zs = (self.z + 8 - self.y - d) % 4
        xs = self.across(a)
        xh2 = self.mid * a + (1 - self.mid) * self.xh
        brick = self.device(self.z, xh2, c2, zs, xs // 2)
        return brick, self.c * 8 + self.y * 2 + xs % 2

    def way_back(self, i, c2):
        d, e = self.step(i)
        y2 = (self.y + self.z + d) % 4
        pair = c2 * 8 + y2 * 2 + (self.xh + e) % 2
        return pair, (self.n * 2 + c2, pair % 8)


def coeffs(labels, index, table):
    return [table[index[labels[level]]] for level in range(4)]


def depth_change(field):
    lane = lax.broadcasted_iota(jnp.int32, field.shape, field.ndim - 1)
    up = jnp.where(lane == 127, 0.0, pltpu.roll(field, 127, field.ndim - 1))
    down = jnp.where(lane == 0, 0.0, pltpu.roll(field, 1, field.ndim - 1))
    return up - down


def cross(p, q):
    return (p[1] * q[2] - p[2] * q[1], p[2] * q[0] - p[0] * q[2], p[0] * q[1] - p[1] * q[0])


def forces_kernel(
    grav_levels,
    grav_step,
    seis_levels,
    seis_step,
    labels_in,
    dens_index_in,
    vel_index_in,
    dens_table_in,
    vel_table_in,
    dens_out,
    vel_out,
    grav_slope,
    seis_slope,
    labels,
    dens_index,
    vel_index,
    dens_table,
    vel_table,
    gl,
    gs,
    sl,
    st,
    sb,
    hb,
    rb,
    db,
    xs,
    xr,
    ys,
    yr,
    cs,
    cr,
    grads,
    edge_grads,
    mixes,
    edge_mixes,
    q1e,
    q1s,
    q2s,
    acc,
    df,
    rs,
    rv,
    load_sem,
    leg1_send,
    leg1_recv,
    leg2_send,
    leg2_recv,
    xh_send,
    xh_recv,
    yd_send,
    yd_recv,
    co_send,
    co_recv,
    yv_send,
    yv_recv,
    ret_send,
    ret_recv,
):
    me = Place()
    slab_rows = seis_levels.shape[1]

    loads = []
    for number, (source, target) in enumerate(
        [
            (labels_in, labels),
            (dens_index_in, dens_index),
            (vel_index_in, vel_index),
            (dens_table_in, dens_table),
            (vel_table_in, vel_table),
            (seis_levels, sl.at[:, pl.ds(PAD, slab_rows), :]),
            (seis_step, st.at[:, pl.ds(PAD, slab_rows), :]),
            (grav_levels, gl),
            (grav_step, gs),
        ]
    ):
        copy = pltpu.make_async_copy(source, target, load_sem.at[number])
        copy.start()
        loads.append(copy)

    barrier = pltpu.get_barrier_semaphore()

    def greet(device):
        pl.semaphore_signal(barrier, inc=1, device_id=device, device_id_type=MESH)

    for dz in range(1, 4):
        greet(me.device((me.z + dz) % 4, me.xh, me.c, me.y, me.xl))

    @pl.when(me.mid == 0)
    def _():
        for z2 in range(4):
            greet(me.device(z2, 1 - me.xh, me.c, me.y, 1 - me.xl))

    for far in range(2):
        x2 = 3 * me.xh if far else 1 + me.xl
        for y2 in range(4):
            for c2 in range(2):
                device = me.device(me.z, x2 // 2, c2, y2, x2 % 2)
                if far:

                    @pl.when(jnp.logical_not(me.is_me(device)))
                    def _():
                        greet(device)

                else:
                    greet(device)

    has_low_x, has_high_x = me.w > 0, me.w < 15
    has_low_y, has_high_y = me.n > 0, me.n < 7
    low_x, high_x = (me.w - 1, me.n), (me.w + 1, me.n)
    low_y, high_y = (me.w, me.n - 1), (me.w, me.n + 1)
    sides = ((has_low_x, low_x), (has_high_x, high_x), (has_low_y, low_y), (has_high_y, high_y))
    corners = [
        (both(sides[sx][0], sides[2 + sy][0]), (me.w + 2 * sx - 1, me.n + 2 * sy - 1))
        for sx in range(2)
        for sy in range(2)
    ]
    for here, device in (*sides, *corners):

        @pl.when(here)
        def _():
            greet(device)

    expected = 3 + 4 * (1 - me.mid) + 15 + me.mid
    for here, _ in (*sides, *corners):
        expected = expected + here.astype(jnp.int32)

    for copy in loads[:5]:
        copy.wait()
    dens_coeff = [0.5 * v for v in coeffs(labels, dens_index, dens_table)]
    vel_coeff = [0.5 * v for v in coeffs(labels, vel_index, vel_table)]

    def remote(source, target, send, recv, device):
        return pltpu.make_async_remote_copy(
            src_ref=source,
            dst_ref=target,
            send_sem=send,
            recv_sem=recv,
            device_id=device,
            device_id_type=MESH,
        )

    def start_any(source, target, send, recv, device):
        mine = me.is_me(device)

        @pl.when(mine)
        def _():
            pltpu.make_async_copy(source, target, recv).start()

        @pl.when(jnp.logical_not(mine))
        def _():
            remote(source, target, send, recv, device).start()

    def await_bytes(ref, sem):
        pltpu.make_async_copy(ref, ref, sem).wait()

    def brick_slot(field, slot):
        return rb.at[field, pl.ds(pl.multiple_of((slot + 1) * MSG, 8), MSG), :]

    def send_slabs(field):
        def one(i, _):
            send_slab(field, i)
            return 0

        lax.fori_loop(0, 8, one, 0)

    def send_slab(field, i):
        pair, relay = me.first_leg(i)
        for c2 in range(2):
            block = pair * 2 + c2
            x_at = block * NX - 2 + lax.broadcasted_iota(jnp.int32, (PITCH, 128), 0)
            inside = both(x_at >= 0, x_at < slab_rows // 2)
            for column in range(2):
                rows = pl.ds(block * 2 * NX + PAD - 4 + column, PITCH, stride=2)
                total = None
                for level in range(4):
                    t = jnp.tanh(sl[level, rows, :])
                    if field == 0:
                        term = vel_coeff[level] * (1.0 + t)
                    else:
                        term = (vel_coeff[level] * (1.0 - t * t)) * st[level, rows, :]
                    total = term if total is None else total + term
                sb[field, i, pl.ds((c2 * 2 + column) * PITCH, PITCH), :] = jnp.where(
                    inside, total, 0.0
                )
        start_any(
            sb.at[field, i], hb.at[field, i], leg1_send.at[field], leg1_recv.at[field, i], relay
        )

    def relay_slab(field, i):
        await_bytes(hb.at[field, i], leg1_recv.at[field, i])
        for c2 in range(2):
            brick, slot = me.second_leg(i, c2)
            which = (slot > 0).astype(jnp.int32) + (slot > 14).astype(jnp.int32)
            start_any(
                hb.at[field, i, pl.ds(c2 * MSG, MSG), :],
                brick_slot(field, slot),
                leg2_send.at[field],
                leg2_recv.at[field, which],
                brick,
            )

    loads[5].wait()
    pl.semaphore_wait(barrier, expected)
    send_slabs(0)

    loads[7].wait()
    loads[8].wait()

    def dens_row(x):
        dens, change = None, None
        for level in range(4):
            t = jnp.tanh(gl[level, x])
            term = dens_coeff[level] * (1.0 + t)
            slope = dens_coeff[level] * (1.0 - t * t)
            grav_slope[level, x] = slope * (1.0 / 16.0)
            slope = slope * gs[level, x]
            dens = term if dens is None else dens + term
            change = slope if change is None else change + slope
        rows = pl.ds(2 * PITCH + 2 + x, NY, stride=PITCH)
        db[0, rows, :] = dens
        db[1, rows, :] = change
        return dens, change

    def edge_row(k, _):
        side, row = k // 2, k % 2
        dens, change = dens_row(side * (NX - 2) + row)
        xs[side, pl.ds(pl.multiple_of(row * NY, 8), NY), :] = dens
        xs[side, pl.ds(pl.multiple_of((2 + row) * NY, 8), NY), :] = change
        return 0

    lax.fori_loop(0, 4, edge_row, 0)

    def x_halo(side):
        return remote(
            xs.at[side],
            xr.at[1 - side],
            xh_send.at[side],
            xh_recv.at[1 - side],
            (low_x, high_x)[side],
        )

    for side in range(2):

        @pl.when(sides[side][0])
        def _():
            x_halo(side).start()

    def inner_row(x, _):
        dens_row(x)
        return 0

    lax.fori_loop(2, NX - 2, inner_row, 0)

    for side in range(2):
        for field in range(2):
            for column in range(2):
                ys[side, pl.ds((field * 2 + column) * NX, NX), :] = db[
                    field, pl.ds((2 + side * (NY - 2) + column) * PITCH + 2, NX), :
                ]
    cs[...] = jnp.zeros(cs.shape, jnp.float32)
    for k in range(4):
        at = (2 + k % 2 * (NY - 1)) * PITCH + 2 + k // 2 * (NX - 1)
        for field in range(2):
            cs[k, pl.ds(field, 1), :] = db[field, pl.ds(at, 1), :]

    def y_side(side):
        return remote(
            ys.at[side], yr.at[1 - side], yd_send.at[side], yd_recv.at[1 - side], sides[2 + side][1]
        )

    def corner(k):
        return remote(cs.at[k], cr.at[3 - k], co_send.at[k], co_recv.at[3 - k], corners[k][1])

    dens_halos = [
        *((sides[side][0], x_halo(side), xr.at[side], xh_recv.at[side]) for side in range(2)),
        *((sides[2 + side][0], y_side(side), yr.at[side], yd_recv.at[side]) for side in range(2)),
        *((corners[k][0], corner(k), cr.at[k], co_recv.at[k]) for k in range(4)),
    ]
    for here, copy, _, _ in dens_halos[2:]:

        @pl.when(here)
        def _():
            copy.start()

    loads[6].wait()

    def relay_and_send(i, _):
        relay_slab(0, i)
        send_slab(1, i)
        return 0

    lax.fori_loop(0, 8, relay_and_send, 0)

    def y_halo(field, side):
        source = rb.at[field, pl.ds((2 + side * (NY - 2)) * PITCH, MSG), :]
        target = rb.at[field, pl.ds((1 - side) * (NY + 2) * PITCH, MSG), :]
        return remote(
            source, target, yv_send.at[field, side], yv_recv.at[field, 1 - side], (low_y, high_y)[side]
        )

    def y_halo_start(field):
        for side in range(2):

            @pl.when(sides[2 + side][0])
            def _():
                y_halo(field, side).start()

            @pl.when(jnp.logical_not(sides[2 + side][0]))
            def _():
                rb[field, pl.ds(side * (NY + 2) * PITCH, MSG), :] = jnp.zeros(
                    (MSG, 128), jnp.float32
                )

    def y_halo_recv(field):
        for side in range(2):

            @pl.when(sides[2 + side][0])
            def _():
                await_bytes(
                    rb.at[field, pl.ds(side * (NY + 2) * PITCH, MSG), :], yv_recv.at[field, side]
                )

    def y_halo_sent(field):
        for side in range(2):

            @pl.when(sides[2 + side][0])
            def _():
                y_halo(field, side).wait_send()

    def y_halo_early(field):
        for slot in (0, 15):
            await_bytes(brick_slot(field, slot), leg2_recv.at[field, slot // 15 * 2])
        y_halo_start(field)

    def relay_second(i, _):
        relay_slab(1, i)
        return 0

    lax.fori_loop(0, 8, relay_second, 0)
    y_halo_early(0)

    for here, _, ref, recv in dens_halos:

        @pl.when(here)
        def _():
            await_bytes(ref, recv)

        @pl.when(jnp.logical_not(here))
        def _():
            ref[...] = jnp.zeros(ref.shape, jnp.float32)

    for field in range(2):
        for side in range(2):
            for row in range(2):
                db[field, pl.ds(2 * PITCH + side * (NX + 2) + row, NY, stride=PITCH), :] = xr[
                    side, pl.ds((field * 2 + row) * NY, NY), :
                ]
                db[field, pl.ds((side * (NY + 2) + row) * PITCH + 2, NX), :] = yr[
                    side, pl.ds((field * 2 + row) * NX, NX), :
                ]
        for k in range(4):
            at = (1 + k % 2 * (NY + 1)) * PITCH + 1 + k // 2 * (NX + 1)
            db[field, pl.ds(at, 1), :] = cr[k, pl.ds(field, 1), :]

    def gradient(ref, field, yy):
        def at(column, x):
            return ref[field, pl.ds(column * PITCH + 2 + x, NX), :]

        return (
            at(yy, 1) - at(yy, -1),
            at(yy + 1, 0) - at(yy - 1, 0),
            depth_change(at(yy, 0)),
        )

    def edge_gradient(ref, field, side, rows):
        x = (-1, NX)[side]

        def at(dy, x):
            start = (rows.start + 2 + dy) * PITCH + 2 + x
            return ref[field, pl.ds(start, rows.size, stride=PITCH), :]

        return (at(0, x + 1) - at(0, x - 1), at(1, x) - at(-1, x), depth_change(at(0, x)))

    every, inner_rows = pl.ds(0, NY), pl.ds(1, NY - 2)

    def keep(ref, *at_and_vector):
        *at, vector = at_and_vector
        for number in range(3):
            ref[(at[0], number, *at[1:])] = vector[number]

    def kept(ref, *at):
        return tuple(ref[(at[0], number, *at[1:])] for number in range(3))

    def columns(body, first, count, batch):
        def some(j, _):
            body([first + j * batch + k for k in range(batch)])
            return 0

        lax.fori_loop(0, count // batch, some, 0)

    def dens_gradient(field):
        def some(yys):
            for yy in yys:
                keep(grads, field, yy, gradient(db, field, yy))

        columns(some, 2, NY, 4)
        some([1, NY + 2])
        for side in range(2):
            keep(edge_grads, field, side, every, edge_gradient(db, field, side, every))

    def mixed(field, own, grads, *at):
        first = cross(kept(grads, 0, *at), own)
        if field == 0:
            return first
        second = cross(kept(grads, 1, *at), kept(grads, 2, *at))
        return tuple(s + t for s, t in zip(second, first))

    def masked(vector, inside):
        factor = inside.astype(jnp.float32)
        return tuple(v * factor for v in vector)

    def vel_columns(field, yys, inside=None):
        qs = []
        for number, yy in enumerate(yys):
            own = gradient(rb, field, yy)
            mix = mixed(field, own, grads, yy)
            if inside is not None:
                mix = masked(mix, inside[number])
            keep(grads, 2 + field, yy, own)
            keep(mixes, field, yy, mix)
            qs.append(cross(mix, kept(grads, 0, yy)))
        collect(qs, yys)

    def vel_edges(field, rows):
        for side in range(2):
            own = edge_gradient(rb, field, side, rows)
            mix = masked(mixed(field, own, edge_grads, side, rows), sides[side][0])
            keep(edge_grads, 2 + field, side, rows, own)
            keep(edge_mixes, field, side, rows, mix)
            dens = kept(edge_grads, 0, side, rows)
            q1e[side, rows] = mix[1] * dens[2] - mix[2] * dens[1]

    def dens_columns(field, yys):
        collect([cross(kept(grads, 2, yy), kept(mixes, field, yy)) for yy in yys], yys)

    def dens_edges(field):
        for side in range(2):
            vel, mix = kept(edge_grads, 2, side, every), kept(edge_mixes, field, side, every)
            q1e[side] = vel[1] * mix[2] - vel[2] * mix[1]

    def collect(qs, yys):
        for k, (q, yy) in enumerate(zip(qs, yys)):
            y = jnp.clip(yy - 2, 0, NY - 1)
            q1s[k, pl.ds(8, NX), :] = q[0]
            q1s[k, pl.ds(7, 1), :] = q1e[0, pl.ds(y, 1), :]
            q1s[k, pl.ds(8 + NX, 1), :] = q1e[1, pl.ds(y, 1), :]
            q2s[yy] = q[1]
        turned = [depth_change(q[2]) for q in qs]
        for k, yy in enumerate(yys):
            acc[yy] = q1s[k, pl.ds(7, NX), :] - q1s[k, pl.ds(9, NX), :] - turned[k]

    def adjoint(yy):
        return acc[yy] + (q2s[yy - 1] - q2s[yy + 1])

    def compute(field):
        vel_edges(field, inner_rows)

        columns(lambda yys: vel_columns(field, yys), 3, NY - 2, 5)
        if field == 0:
            y_halo_early(1)
        y_halo_recv(field)
        vel_edges(field, every)
        true = me.n >= 0
        vel_columns(field, [1, 2, NY + 1, NY + 2], [me.n > 0, true, true, me.n < 7])

        def back(i, _):
            for c2 in range(2):
                p, slab = me.way_back(i, c2)
                for half in range(2):
                    rs[field, p, pl.ds(half * NX, NX), :] = adjoint(2 * p + 2 + half)
                start_any(
                    rs.at[field, p], rv.at[field, me.w], ret_send.at[field], ret_recv.at[field], slab
                )
            return 0

        lax.fori_loop(0, 8, back, 0)

    def arrive(field):
        await_bytes(rb.at[field, pl.ds(2 * MSG, 14 * MSG), :], leg2_recv.at[field, 1])

    for field in range(2):
        dens_gradient(field)
    arrive(0)
    compute(0)
    arrive(1)
    compute(1)

    for field in range(2):
        dens_edges(field)

        columns(lambda yys: dens_columns(field, yys), 2, NY, 4)
        dens_columns(field, [1, NY + 2])

        def keep_force(y, _):
            for k in range(4):
                at = pl.ds(pl.multiple_of((4 * y + k) * NX, 8), NX)
                df[field, at, :] = adjoint(4 * y + k + 2)
            return 0

        lax.fori_loop(0, NY // 4, keep_force, 0)

    for field in range(2):

        def turn(x, _):
            dens_out[field, x] = df[field, pl.ds(x, NY, stride=NX), :]
            return 0

        lax.fori_loop(0, NX, turn, 0)

    def seis_rows(i, _):
        for level in range(4):
            t = jnp.tanh(sl[level, pl.ds(pl.multiple_of(PAD + i * 32, 8), 32), :])
            scale = vel_coeff[level] * (1.0 / 16.0)
            seis_slope[level, pl.ds(pl.multiple_of(i * 32, 8), 32), :] = scale * (1.0 - t * t)
        return 0

    lax.fori_loop(0, slab_rows // 32, seis_rows, 0)

    for field in range(2):

        await_bytes(rv.at[field], ret_recv.at[field])

        def finish(block, _):
            for half in range(2):
                vel_out[field, pl.ds(block * 2 * NX + half, NX, stride=2), :] = rv[
                    field, block, pl.ds(half * NX, NX), :
                ]
            return 0

        lax.fori_loop(0, 16, finish, 0)

    for here, copy, _, _ in dens_halos:

        @pl.when(here)
        def _():
            copy.wait_send()

    for field in range(2):
        y_halo_sent(field)

        await_bytes(sb.at[field, pl.ds(0, 6)], leg1_send.at[field])
        await_bytes(rb.at[field, pl.ds(0, 15 * MSG), :], leg2_send.at[field])
        await_bytes(rs.at[field, pl.ds(0, 15)], ret_send.at[field])

        @pl.when(me.mid == 0)
        def _():
            await_bytes(sb.at[field, 0], leg1_send.at[field])

        @pl.when(me.mid == 1)
        def _():
            await_bytes(rb.at[field, pl.ds(0, MSG), :], leg2_send.at[field])

        @pl.when(me.w // 2 != me.n)
        def _():
            await_bytes(rs.at[field, 0], ret_send.at[field])


def chain_kernel(
    steps,
    dens_force,
    vel_force,
    grav_slope,
    seis_slope,
    grav_gradient,
    grav_curvature,
    seis_gradient,
    seis_curvature,
):
    for slope, force, outs in (
        (grav_slope, dens_force, (grav_gradient, grav_curvature)),
        (seis_slope, vel_force, (seis_gradient, seis_curvature)),
    ):
        rows = slope.shape[1] // steps
        here = pl.ds(pl.program_id(0) * rows, rows)
        for level in range(4):
            factor = slope[level, here]
            for number in range(2):
                outs[number][level] = factor * force[number, here]


def shards(
    grav_levels,
    grav_step,
    seis_levels,
    seis_step,
    unit_labels,
    dens_index,
    vel_index,
    dens_table,
    vel_table,
):
    levels, nx, ny, nz = grav_levels.shape
    slab_x, slab_y = seis_levels.shape[1:3]
    rows = slab_x * slab_y
    seis_rows = seis_levels.reshape(levels, rows, nz)
    step_rows = seis_step.reshape(levels, rows, nz)
    tables = (unit_labels, dens_index, vel_index, dens_table, vel_table)
    hbm = pl.BlockSpec(memory_space=pltpu.HBM)
    vmem = pl.BlockSpec(memory_space=pltpu.VMEM)
    f32 = jnp.float32
    dma = pltpu.SemaphoreType.DMA
    brick_shape = jax.ShapeDtypeStruct(grav_levels.shape, f32)
    slab_shape = jax.ShapeDtypeStruct(seis_rows.shape, f32)
    forces = pl.pallas_call(
        forces_kernel,
        out_shape=(
            jax.ShapeDtypeStruct((2, nx, ny, nz), f32),
            jax.ShapeDtypeStruct((2, rows, nz), f32),
            brick_shape,
            slab_shape,
        ),
        in_specs=[hbm] * 9,
        out_specs=(vmem,) * 4,
        scratch_shapes=[
            *(pltpu.SMEM(table.shape, table.dtype) for table in tables),
            pltpu.VMEM((levels, nx, ny, nz), f32),
            pltpu.VMEM((levels, nx, ny, nz), f32),
            pltpu.VMEM((levels, rows + 4 * PAD, nz), f32),
            pltpu.VMEM((levels, rows + 4 * PAD, nz), f32),
            pltpu.VMEM((2, 8, 2 * MSG, nz), f32),
            pltpu.VMEM((2, 8, 2 * MSG, nz), f32),
            pltpu.VMEM((2, COLS, nz), f32),
            pltpu.VMEM((2, COLS, nz), f32),
            pltpu.VMEM((2, 4 * NY, nz), f32),
            pltpu.VMEM((2, 4 * NY, nz), f32),
            pltpu.VMEM((2, 4 * NX, nz), f32),
            pltpu.VMEM((2, 4 * NX, nz), f32),
            pltpu.VMEM((4, 8, nz), f32),
            pltpu.VMEM((4, 8, nz), f32),
            pltpu.VMEM((4, 3, NY + 4, NX, nz), f32),
            pltpu.VMEM((4, 3, 2, NY, nz), f32),
            pltpu.VMEM((2, 3, NY + 4, NX, nz), f32),
            pltpu.VMEM((2, 3, 2, NY, nz), f32),
            pltpu.VMEM((2, NY, nz), f32),
            pltpu.VMEM((5, NX + 16, nz), f32),
            pltpu.VMEM((NY + 4, NX, nz), f32),
            pltpu.VMEM((NY + 4, NX, nz), f32),
            pltpu.VMEM((2, NY * NX, nz), f32),
            pltpu.VMEM((2, 16, 2 * NX, nz), f32),
            pltpu.VMEM((2, 16, 2 * NX, nz), f32),
            dma((9,)),
            dma((2,)),
            dma((2, 8)),
            dma((2,)),
            dma((2, 3)),
            dma((2,)),
            dma((2,)),
            dma((2,)),
            dma((2,)),
            dma((4,)),
            dma((4,)),
            dma((2, 2)),
            dma((2, 2)),
            dma((2,)),
            dma((2,)),
        ],
        compiler_params=pltpu.CompilerParams(
            collective_id=0, has_side_effects=True, vmem_limit_bytes=42 << 20
        ),
        name="forces",
    )(*(pltpu.with_memory_space_constraint(v, pltpu.HBM) for v in (grav_levels, grav_step, seis_rows, step_rows, *tables)))

    steps = 8
    brick = pl.BlockSpec((levels, nx // steps, ny, nz), lambda i: (0, i, 0, 0))
    slab = pl.BlockSpec((levels, rows // steps, nz), lambda i: (0, i, 0))
    outs = pl.pallas_call(
        functools.partial(chain_kernel, steps),
        grid=(steps,),
        out_shape=(brick_shape, brick_shape, slab_shape, slab_shape),
        in_specs=[vmem] * 4,
        out_specs=(brick, brick, slab, slab),
        compiler_params=pltpu.CompilerParams(vmem_limit_bytes=32 << 20),
        name="chain",
    )(*forces)
    return (
        outs[0],
        outs[1],
        outs[2].reshape(seis_levels.shape),
        outs[3].reshape(seis_levels.shape),
    )


def solution(mesh):
    placed = (
        P(None, "wide", "narrow", None),
        P(None, "wide", "narrow", None),
        P(None, None, ("wide", "narrow"), None),
        P(None, None, ("wide", "narrow"), None),
        P(),
        P(),
        P(),
        P(),
        P(),
    )
    return jax.shard_map(
        shards,
        mesh=mesh,
        in_specs=placed,
        out_specs=placed[:4],
        check_vma=False,
    )
```

```python
import functools

import jax
import jax.numpy as jnp
from jax import lax
from jax.experimental import pallas as pl
from jax.experimental.pallas import tpu as pltpu
from jax.sharding import PartitionSpec as P

MESH = pl.DeviceIdType.MESH
NX = 32
NY = 32
PITCH = NX + 4
MSG = 2 * PITCH
COLS = (NY + 4) * PITCH
PAD = 8


def both(one, other):
    return jnp.logical_and(one, other)


class Place:
    def __init__(self):
        self.w = lax.axis_index("wide")
        self.n = lax.axis_index("narrow")
        self.z = self.w // 4
        self.xh = (self.w // 2) % 2
        self.c = self.w % 2
        self.y = self.n // 2
        self.xl = self.n % 2
        self.x = self.xh * 2 + self.xl
        self.mid = (self.xh + self.xl) % 2

    @staticmethod
    def device(z, xh, c, y, xl):
        return (z * 4 + xh * 2 + c, y * 2 + xl)

    def is_me(self, device):
        return both(device[0] == self.w, device[1] == self.n)

    def across(self, a):
        return self.x + (1 - self.mid) * a * (3 - 2 * self.x)

    def step(self, i):
        pair, half = i // 2, i % 2
        return pair // 2 + 2 * half, (pair + half) % 2

    def side(self, e):
        return 1 - e + (1 - self.xh) * self.xl * (2 * e - 1)

    def first_leg(self, i):
        d, e = self.step(i)
        a = self.side(e)
        z2 = (self.z + self.y + d) % 4
        xr = self.across(a)
        xh2 = self.mid * a + (1 - self.mid) * (xr // 2)
        return z2 * 2 + xh2, self.device(z2, xr // 2, self.c, self.y, xr % 2)

    def second_leg(self, i, c2):
        d, e = self.step(i)
        a = self.side(e)
        zs = (self.z + 8 - self.y - d) % 4
        xs = self.across(a)
        xh2 = self.mid * a + (1 - self.mid) * self.xh
        brick = self.device(self.z, xh2, c2, zs, xs // 2)
        return brick, self.c * 8 + self.y * 2 + xs % 2

    def way_back(self, i, c2):
        d, e = self.step(i)
        y2 = (self.y + self.z + d) % 4
        pair = c2 * 8 + y2 * 2 + (self.xh + e) % 2
        return pair, (self.n * 2 + c2, pair % 8)


def coeffs(labels, index, table):
    return [table[index[labels[level]]] for level in range(4)]


def depth_change(field):
    lane = lax.broadcasted_iota(jnp.int32, field.shape, field.ndim - 1)
    up = jnp.where(lane == 127, 0.0, pltpu.roll(field, 127, field.ndim - 1))
    down = jnp.where(lane == 0, 0.0, pltpu.roll(field, 1, field.ndim - 1))
    return up - down


def cross(p, q):
    return (p[1] * q[2] - p[2] * q[1], p[2] * q[0] - p[0] * q[2], p[0] * q[1] - p[1] * q[0])


def forces_kernel(
    grav_levels,
    grav_step,
    seis_levels,
    seis_step,
    labels_in,
    dens_index_in,
    vel_index_in,
    dens_table_in,
    vel_table_in,
    dens_out,
    vel_out,
    grav_slope,
    seis_slope,
    labels,
    dens_index,
    vel_index,
    dens_table,
    vel_table,
    gl,
    gs,
    sl,
    st,
    sb,
    hb,
    rb,
    db,
    xs,
    xr,
    ys,
    yr,
    cs,
    cr,
    grads,
    edge_grads,
    mixes,
    edge_mixes,
    q1e,
    q1s,
    q2s,
    acc,
    df,
    rs,
    rv,
    load_sem,
    leg1_send,
    leg1_recv,
    leg2_send,
    leg2_recv,
    xh_send,
    xh_recv,
    yd_send,
    yd_recv,
    co_send,
    co_recv,
    yv_send,
    yv_recv,
    ret_send,
    ret_recv,
):
    me = Place()
    slab_rows = seis_levels.shape[1]

    loads = []
    for number, (source, target) in enumerate(
        [
            (seis_levels, sl.at[:, pl.ds(PAD, slab_rows), :]),
            (labels_in, labels),
            (dens_index_in, dens_index),
            (vel_index_in, vel_index),
            (dens_table_in, dens_table),
            (vel_table_in, vel_table),
            (seis_step, st.at[:, pl.ds(PAD, slab_rows), :]),
            (grav_levels, gl),
            (grav_step, gs),
        ]
    ):
        copy = pltpu.make_async_copy(source, target, load_sem.at[number])
        copy.start()
        loads.append(copy)

    barrier = pltpu.get_barrier_semaphore()

    def greet(device):
        pl.semaphore_signal(barrier, inc=1, device_id=device, device_id_type=MESH)

    for dz in range(1, 4):
        greet(me.device((me.z + dz) % 4, me.xh, me.c, me.y, me.xl))

    @pl.when(me.mid == 0)
    def _():
        for z2 in range(4):
            greet(me.device(z2, 1 - me.xh, me.c, me.y, 1 - me.xl))

    for far in range(2):
        x2 = 3 * me.xh if far else 1 + me.xl
        for y2 in range(4):
            for c2 in range(2):
                device = me.device(me.z, x2 // 2, c2, y2, x2 % 2)
                if far:

                    @pl.when(jnp.logical_not(me.is_me(device)))
                    def _():
                        greet(device)

                else:
                    greet(device)

    has_low_x, has_high_x = me.w > 0, me.w < 15
    has_low_y, has_high_y = me.n > 0, me.n < 7
    low_x, high_x = (me.w - 1, me.n), (me.w + 1, me.n)
    low_y, high_y = (me.w, me.n - 1), (me.w, me.n + 1)
    sides = ((has_low_x, low_x), (has_high_x, high_x), (has_low_y, low_y), (has_high_y, high_y))
    corners = [
        (both(sides[sx][0], sides[2 + sy][0]), (me.w + 2 * sx - 1, me.n + 2 * sy - 1))
        for sx in range(2)
        for sy in range(2)
    ]
    for here, device in (*sides, *corners):

        @pl.when(here)
        def _():
            greet(device)

    expected = 3 + 4 * (1 - me.mid) + 15 + me.mid
    for here, _ in (*sides, *corners):
        expected = expected + here.astype(jnp.int32)

    for copy in loads[1:6]:
        copy.wait()
    dens_coeff = [0.5 * v for v in coeffs(labels, dens_index, dens_table)]
    vel_coeff = [0.5 * v for v in coeffs(labels, vel_index, vel_table)]

    def remote(source, target, send, recv, device):
        return pltpu.make_async_remote_copy(
            src_ref=source,
            dst_ref=target,
            send_sem=send,
            recv_sem=recv,
            device_id=device,
            device_id_type=MESH,
        )

    def start_any(source, target, send, recv, device):
        mine = me.is_me(device)

        @pl.when(mine)
        def _():
            pltpu.make_async_copy(source, target, recv).start()

        @pl.when(jnp.logical_not(mine))
        def _():
            remote(source, target, send, recv, device).start()

    def await_bytes(ref, sem):
        pltpu.make_async_copy(ref, ref, sem).wait()

    def brick_slot(field, slot):
        return rb.at[field, pl.ds(pl.multiple_of((slot + 1) * MSG, 8), MSG), :]

    def send_slabs(field):
        def one(i, _):
            send_slab(field, i)
            return 0

        lax.fori_loop(0, 8, one, 0)

    def send_slab(field, i):
        pair, relay = me.first_leg(i)
        for c2 in range(2):
            block = pair * 2 + c2
            x_at = block * NX - 2 + lax.broadcasted_iota(jnp.int32, (PITCH, 128), 0)
            inside = both(x_at >= 0, x_at < slab_rows // 2)
            for column in range(2):
                rows = pl.ds(block * 2 * NX + PAD - 4 + column, PITCH, stride=2)
                total = None
                for level in range(4):
                    t = jnp.tanh(sl[level, rows, :])
                    if field == 0:
                        term = vel_coeff[level] * (1.0 + t)
                    else:
                        term = (vel_coeff[level] * (1.0 - t * t)) * st[level, rows, :]
                    total = term if total is None else total + term
                sb[field, i, pl.ds((c2 * 2 + column) * PITCH, PITCH), :] = jnp.where(
                    inside, total, 0.0
                )
        start_any(
            sb.at[field, i], hb.at[field, i], leg1_send.at[field], leg1_recv.at[field, i], relay
        )

    def relay_slab(field, i):
        await_bytes(hb.at[field, i], leg1_recv.at[field, i])
        for c2 in range(2):
            brick, slot = me.second_leg(i, c2)
            which = (slot > 0).astype(jnp.int32) + (slot > 14).astype(jnp.int32)
            start_any(
                hb.at[field, i, pl.ds(c2 * MSG, MSG), :],
                brick_slot(field, slot),
                leg2_send.at[field],
                leg2_recv.at[field, which],
                brick,
            )

    loads[0].wait()
    pl.semaphore_wait(barrier, expected)
    send_slabs(0)

    loads[7].wait()
    loads[8].wait()

    def dens_row(x):
        dens, change = None, None
        for level in range(4):
            t = jnp.tanh(gl[level, x])
            term = dens_coeff[level] * (1.0 + t)
            slope = dens_coeff[level] * (1.0 - t * t)
            grav_slope[level, x] = slope * (1.0 / 16.0)
            slope = slope * gs[level, x]
            dens = term if dens is None else dens + term
            change = slope if change is None else change + slope
        rows = pl.ds(2 * PITCH + 2 + x, NY, stride=PITCH)
        db[0, rows, :] = dens
        db[1, rows, :] = change
        return dens, change

    def edge_row(k, _):
        side, row = k // 2, k % 2
        dens, change = dens_row(side * (NX - 2) + row)
        xs[side, pl.ds(pl.multiple_of(row * NY, 8), NY), :] = dens
        xs[side, pl.ds(pl.multiple_of((2 + row) * NY, 8), NY), :] = change
        return 0

    lax.fori_loop(0, 4, edge_row, 0)

    def x_halo(side):
        return remote(
            xs.at[side],
            xr.at[1 - side],
            xh_send.at[side],
            xh_recv.at[1 - side],
            (low_x, high_x)[side],
        )

    for side in range(2):

        @pl.when(sides[side][0])
        def _():
            x_halo(side).start()

    def inner_row(x, _):
        dens_row(x)
        return 0

    lax.fori_loop(2, NX - 2, inner_row, 0)

    for side in range(2):
        for field in range(2):
            for column in range(2):
                ys[side, pl.ds((field * 2 + column) * NX, NX), :] = db[
                    field, pl.ds((2 + side * (NY - 2) + column) * PITCH + 2, NX), :
                ]
    cs[...] = jnp.zeros(cs.shape, jnp.float32)
    for k in range(4):
        at = (2 + k % 2 * (NY - 1)) * PITCH + 2 + k // 2 * (NX - 1)
        for field in range(2):
            cs[k, pl.ds(field, 1), :] = db[field, pl.ds(at, 1), :]

    def y_side(side):
        return remote(
            ys.at[side], yr.at[1 - side], yd_send.at[side], yd_recv.at[1 - side], sides[2 + side][1]
        )

    def corner(k):
        return remote(cs.at[k], cr.at[3 - k], co_send.at[k], co_recv.at[3 - k], corners[k][1])

    dens_halos = [
        *((sides[side][0], x_halo(side), xr.at[side], xh_recv.at[side]) for side in range(2)),
        *((sides[2 + side][0], y_side(side), yr.at[side], yd_recv.at[side]) for side in range(2)),
        *((corners[k][0], corner(k), cr.at[k], co_recv.at[k]) for k in range(4)),
    ]
    for here, copy, _, _ in dens_halos[2:]:

        @pl.when(here)
        def _():
            copy.start()

    loads[6].wait()

    def relay_and_send(i, _):
        relay_slab(0, i)
        send_slab(1, i)
        return 0

    lax.fori_loop(0, 8, relay_and_send, 0)

    def y_halo(field, side):
        source = rb.at[field, pl.ds((2 + side * (NY - 2)) * PITCH, MSG), :]
        target = rb.at[field, pl.ds((1 - side) * (NY + 2) * PITCH, MSG), :]
        return remote(
            source, target, yv_send.at[field, side], yv_recv.at[field, 1 - side], (low_y, high_y)[side]
        )

    def y_halo_start(field):
        for side in range(2):

            @pl.when(sides[2 + side][0])
            def _():
                y_halo(field, side).start()

            @pl.when(jnp.logical_not(sides[2 + side][0]))
            def _():
                rb[field, pl.ds(side * (NY + 2) * PITCH, MSG), :] = jnp.zeros(
                    (MSG, 128), jnp.float32
                )

    def y_halo_recv(field):
        for side in range(2):

            @pl.when(sides[2 + side][0])
            def _():
                await_bytes(
                    rb.at[field, pl.ds(side * (NY + 2) * PITCH, MSG), :], yv_recv.at[field, side]
                )

    def y_halo_sent(field):
        for side in range(2):

            @pl.when(sides[2 + side][0])
            def _():
                y_halo(field, side).wait_send()

    def y_halo_early(field):
        for slot in (0, 15):
            await_bytes(brick_slot(field, slot), leg2_recv.at[field, slot // 15 * 2])
        y_halo_start(field)

    def relay_second(i, _):
        relay_slab(1, i)
        return 0

    lax.fori_loop(0, 8, relay_second, 0)
    y_halo_early(0)

    for here, _, ref, recv in dens_halos:

        @pl.when(here)
        def _():
            await_bytes(ref, recv)

        @pl.when(jnp.logical_not(here))
        def _():
            ref[...] = jnp.zeros(ref.shape, jnp.float32)

    for field in range(2):
        for side in range(2):
            for row in range(2):
                db[field, pl.ds(2 * PITCH + side * (NX + 2) + row, NY, stride=PITCH), :] = xr[
                    side, pl.ds((field * 2 + row) * NY, NY), :
                ]
                db[field, pl.ds((side * (NY + 2) + row) * PITCH + 2, NX), :] = yr[
                    side, pl.ds((field * 2 + row) * NX, NX), :
                ]
        for k in range(4):
            at = (1 + k % 2 * (NY + 1)) * PITCH + 1 + k // 2 * (NX + 1)
            db[field, pl.ds(at, 1), :] = cr[k, pl.ds(field, 1), :]

    def gradient(ref, field, yy):
        def at(column, x):
            return ref[field, pl.ds(column * PITCH + 2 + x, NX), :]

        return (
            at(yy, 1) - at(yy, -1),
            at(yy + 1, 0) - at(yy - 1, 0),
            depth_change(at(yy, 0)),
        )

    def edge_gradient(ref, field, side, rows):
        x = (-1, NX)[side]

        def at(dy, x):
            start = (rows.start + 2 + dy) * PITCH + 2 + x
            return ref[field, pl.ds(start, rows.size, stride=PITCH), :]

        return (at(0, x + 1) - at(0, x - 1), at(1, x) - at(-1, x), depth_change(at(0, x)))

    every, inner_rows = pl.ds(0, NY), pl.ds(1, NY - 2)

    def keep(ref, *at_and_vector):
        *at, vector = at_and_vector
        for number in range(3):
            ref[(at[0], number, *at[1:])] = vector[number]

    def kept(ref, *at):
        return tuple(ref[(at[0], number, *at[1:])] for number in range(3))

    def columns(body, first, count, batch):
        def some(j, _):
            body([first + j * batch + k for k in range(batch)])
            return 0

        lax.fori_loop(0, count // batch, some, 0)

    def dens_gradient(field):
        def some(yys):
            for yy in yys:
                keep(grads, field, yy, gradient(db, field, yy))

        columns(some, 2, NY, 4)
        some([1, NY + 2])
        for side in range(2):
            keep(edge_grads, field, side, every, edge_gradient(db, field, side, every))

    def mixed(field, own, grads, *at):
        first = cross(kept(grads, 0, *at), own)
        if field == 0:
            return first
        second = cross(kept(grads, 1, *at), kept(grads, 2, *at))
        return tuple(s + t for s, t in zip(second, first))

    def masked(vector, inside):
        factor = inside.astype(jnp.float32)
        return tuple(v * factor for v in vector)

    def vel_columns(field, yys, inside=None):
        qs = []
        for number, yy in enumerate(yys):
            own = gradient(rb, field, yy)
            mix = mixed(field, own, grads, yy)
            if inside is not None:
                mix = masked(mix, inside[number])
            keep(grads, 2 + field, yy, own)
            keep(mixes, field, yy, mix)
            qs.append(cross(mix, kept(grads, 0, yy)))
        collect(qs, yys)

    def vel_edges(field, rows):
        for side in range(2):
            own = edge_gradient(rb, field, side, rows)
            mix = masked(mixed(field, own, edge_grads, side, rows), sides[side][0])
            keep(edge_grads, 2 + field, side, rows, own)
            keep(edge_mixes, field, side, rows, mix)
            dens = kept(edge_grads, 0, side, rows)
            q1e[side, rows] = mix[1] * dens[2] - mix[2] * dens[1]

    def dens_columns(field, yys):
        collect([cross(kept(grads, 2, yy), kept(mixes, field, yy)) for yy in yys], yys)

    def dens_edges(field):
        for side in range(2):
            vel, mix = kept(edge_grads, 2, side, every), kept(edge_mixes, field, side, every)
            q1e[side] = vel[1] * mix[2] - vel[2] * mix[1]

    def collect(qs, yys):
        for k, (q, yy) in enumerate(zip(qs, yys)):
            y = jnp.clip(yy - 2, 0, NY - 1)
            q1s[k, pl.ds(8, NX), :] = q[0]
            q1s[k, pl.ds(7, 1), :] = q1e[0, pl.ds(y, 1), :]
            q1s[k, pl.ds(8 + NX, 1), :] = q1e[1, pl.ds(y, 1), :]
            q2s[yy] = q[1]
        turned = [depth_change(q[2]) for q in qs]
        for k, yy in enumerate(yys):
            acc[yy] = q1s[k, pl.ds(7, NX), :] - q1s[k, pl.ds(9, NX), :] - turned[k]

    def adjoint(yy):
        return acc[yy] + (q2s[yy - 1] - q2s[yy + 1])

    def compute(field):
        vel_edges(field, inner_rows)

        columns(lambda yys: vel_columns(field, yys), 3, NY - 2, 5)
        if field == 0:
            y_halo_early(1)
        y_halo_recv(field)
        vel_edges(field, every)
        true = me.n >= 0
        vel_columns(field, [1, 2, NY + 1, NY + 2], [me.n > 0, true, true, me.n < 7])

        def back(i, _):
            for c2 in range(2):
                p, slab = me.way_back(i, c2)
                for half in range(2):
                    rs[field, p, pl.ds(half * NX, NX), :] = adjoint(2 * p + 2 + half)
                start_any(
                    rs.at[field, p], rv.at[field, me.w], ret_send.at[field], ret_recv.at[field], slab
                )
            return 0

        lax.fori_loop(0, 8, back, 0)

    def arrive(field):
        await_bytes(rb.at[field, pl.ds(2 * MSG, 14 * MSG), :], leg2_recv.at[field, 1])

    for field in range(2):
        dens_gradient(field)
    arrive(0)
    compute(0)
    arrive(1)
    compute(1)

    for field in range(2):
        dens_edges(field)

        columns(lambda yys: dens_columns(field, yys), 2, NY, 4)
        dens_columns(field, [1, NY + 2])

        def keep_force(y, _):
            for k in range(4):
                at = pl.ds(pl.multiple_of((4 * y + k) * NX, 8), NX)
                df[field, at, :] = adjoint(4 * y + k + 2)
            return 0

        lax.fori_loop(0, NY // 4, keep_force, 0)

    for field in range(2):

        def turn(x, _):
            dens_out[field, x] = df[field, pl.ds(x, NY, stride=NX), :]
            return 0

        lax.fori_loop(0, NX, turn, 0)

    def seis_rows(i, _):
        for level in range(4):
            t = jnp.tanh(sl[level, pl.ds(pl.multiple_of(PAD + i * 32, 8), 32), :])
            scale = vel_coeff[level] * (1.0 / 16.0)
            seis_slope[level, pl.ds(pl.multiple_of(i * 32, 8), 32), :] = scale * (1.0 - t * t)
        return 0

    lax.fori_loop(0, slab_rows // 32, seis_rows, 0)

    for field in range(2):

        await_bytes(rv.at[field], ret_recv.at[field])

        def finish(block, _):
            for half in range(2):
                vel_out[field, pl.ds(block * 2 * NX + half, NX, stride=2), :] = rv[
                    field, block, pl.ds(half * NX, NX), :
                ]
            return 0

        lax.fori_loop(0, 16, finish, 0)

    for here, copy, _, _ in dens_halos:

        @pl.when(here)
        def _():
            copy.wait_send()

    for field in range(2):
        y_halo_sent(field)

        await_bytes(sb.at[field, pl.ds(0, 6)], leg1_send.at[field])
        await_bytes(rb.at[field, pl.ds(0, 15 * MSG), :], leg2_send.at[field])
        await_bytes(rs.at[field, pl.ds(0, 15)], ret_send.at[field])

        @pl.when(me.mid == 0)
        def _():
            await_bytes(sb.at[field, 0], leg1_send.at[field])

        @pl.when(me.mid == 1)
        def _():
            await_bytes(rb.at[field, pl.ds(0, MSG), :], leg2_send.at[field])

        @pl.when(me.w // 2 != me.n)
        def _():
            await_bytes(rs.at[field, 0], ret_send.at[field])


def chain_kernel(
    steps,
    dens_force,
    vel_force,
    grav_slope,
    seis_slope,
    grav_gradient,
    grav_curvature,
    seis_gradient,
    seis_curvature,
    brick_outs,
    slab_outs,
    sems,
):
    parts = (
        (grav_slope, dens_force, (grav_gradient, grav_curvature), brick_outs, 0),
        (seis_slope, vel_force, (seis_gradient, seis_curvature), slab_outs, 2),
    )

    def step(i, _):
        for slope, force, outs, made, sem in parts:
            rows = slope.shape[1] // steps
            here = pl.ds(i * rows, rows)
            for level in range(4):
                factor = slope[level, here]
                for number in range(2):
                    made[number, level, here] = factor * force[number, here]
            for number in range(2):
                pltpu.make_async_copy(
                    made.at[number, :, here], outs[number].at[:, here], sems.at[sem + number]
                ).start()
        return 0

    lax.fori_loop(0, steps, step, 0)
    for _, _, outs, made, sem in parts:
        for number in range(2):
            pltpu.make_async_copy(made.at[number], outs[number], sems.at[sem + number]).wait()


def shards(
    grav_levels,
    grav_step,
    seis_levels,
    seis_step,
    unit_labels,
    dens_index,
    vel_index,
    dens_table,
    vel_table,
):
    levels, nx, ny, nz = grav_levels.shape
    slab_x, slab_y = seis_levels.shape[1:3]
    rows = slab_x * slab_y
    seis_rows = seis_levels.reshape(levels, rows, nz)
    step_rows = seis_step.reshape(levels, rows, nz)
    tables = (unit_labels, dens_index, vel_index, dens_table, vel_table)
    hbm = pl.BlockSpec(memory_space=pltpu.HBM)
    vmem = pl.BlockSpec(memory_space=pltpu.VMEM)
    f32 = jnp.float32
    dma = pltpu.SemaphoreType.DMA
    brick_shape = jax.ShapeDtypeStruct(grav_levels.shape, f32)
    slab_shape = jax.ShapeDtypeStruct(seis_rows.shape, f32)
    forces = pl.pallas_call(
        forces_kernel,
        out_shape=(
            jax.ShapeDtypeStruct((2, nx, ny, nz), f32),
            jax.ShapeDtypeStruct((2, rows, nz), f32),
            brick_shape,
            slab_shape,
        ),
        in_specs=[hbm] * 9,
        out_specs=(vmem,) * 4,
        scratch_shapes=[
            *(pltpu.SMEM(table.shape, table.dtype) for table in tables),
            pltpu.VMEM((levels, nx, ny, nz), f32),
            pltpu.VMEM((levels, nx, ny, nz), f32),
            pltpu.VMEM((levels, rows + 4 * PAD, nz), f32),
            pltpu.VMEM((levels, rows + 4 * PAD, nz), f32),
            pltpu.VMEM((2, 8, 2 * MSG, nz), f32),
            pltpu.VMEM((2, 8, 2 * MSG, nz), f32),
            pltpu.VMEM((2, COLS, nz), f32),
            pltpu.VMEM((2, COLS, nz), f32),
            pltpu.VMEM((2, 4 * NY, nz), f32),
            pltpu.VMEM((2, 4 * NY, nz), f32),
            pltpu.VMEM((2, 4 * NX, nz), f32),
            pltpu.VMEM((2, 4 * NX, nz), f32),
            pltpu.VMEM((4, 8, nz), f32),
            pltpu.VMEM((4, 8, nz), f32),
            pltpu.VMEM((4, 3, NY + 4, NX, nz), f32),
            pltpu.VMEM((4, 3, 2, NY, nz), f32),
            pltpu.VMEM((2, 3, NY + 4, NX, nz), f32),
            pltpu.VMEM((2, 3, 2, NY, nz), f32),
            pltpu.VMEM((2, NY, nz), f32),
            pltpu.VMEM((5, NX + 16, nz), f32),
            pltpu.VMEM((NY + 4, NX, nz), f32),
            pltpu.VMEM((NY + 4, NX, nz), f32),
            pltpu.VMEM((2, NY * NX, nz), f32),
            pltpu.VMEM((2, 16, 2 * NX, nz), f32),
            pltpu.VMEM((2, 16, 2 * NX, nz), f32),
            dma((9,)),
            dma((2,)),
            dma((2, 8)),
            dma((2,)),
            dma((2, 3)),
            dma((2,)),
            dma((2,)),
            dma((2,)),
            dma((2,)),
            dma((4,)),
            dma((4,)),
            dma((2, 2)),
            dma((2, 2)),
            dma((2,)),
            dma((2,)),
        ],
        compiler_params=pltpu.CompilerParams(
            collective_id=0, has_side_effects=True, vmem_limit_bytes=42 << 20
        ),
        name="forces",
    )(*(pltpu.with_memory_space_constraint(v, pltpu.HBM) for v in (grav_levels, grav_step, seis_rows, step_rows, *tables)))

    outs = pl.pallas_call(
        functools.partial(chain_kernel, 8),
        out_shape=(brick_shape, brick_shape, slab_shape, slab_shape),
        in_specs=[vmem] * 4,
        out_specs=(hbm,) * 4,
        scratch_shapes=[
            pltpu.VMEM((2, *brick_shape.shape), f32),
            pltpu.VMEM((2, *slab_shape.shape), f32),
            dma((4,)),
        ],
        compiler_params=pltpu.CompilerParams(vmem_limit_bytes=32 << 20),
        name="chain",
    )(*forces)
    return (
        outs[0],
        outs[1],
        outs[2].reshape(seis_levels.shape),
        outs[3].reshape(seis_levels.shape),
    )


def solution(mesh):
    placed = (
        P(None, "wide", "narrow", None),
        P(None, "wide", "narrow", None),
        P(None, None, ("wide", "narrow"), None),
        P(None, None, ("wide", "narrow"), None),
        P(),
        P(),
        P(),
        P(),
        P(),
    )
    return jax.shard_map(
        shards,
        mesh=mesh,
        in_specs=placed,
        out_specs=placed[:4],
        check_vma=False,
    )
```

```python
import functools

import jax
import jax.numpy as jnp
from jax import lax
from jax.experimental import pallas as pl
from jax.experimental.pallas import tpu as pltpu
from jax.sharding import PartitionSpec as P

MESH = pl.DeviceIdType.MESH
NX = 32
NY = 32
PITCH = NX + 4
MSG = 2 * PITCH
COLS = (NY + 4) * PITCH
PAD = 8


def quotient(value, by):
    return value // by if isinstance(value, int) else lax.div(value, jnp.int32(by))


def rest(value, by):
    return value % by if isinstance(value, int) else lax.rem(value, jnp.int32(by))


def both(one, other):
    return jnp.logical_and(one, other)


class Place:
    def __init__(self):
        self.w = lax.axis_index("wide")
        self.n = lax.axis_index("narrow")
        self.z = quotient(self.w, 4)
        self.xh = rest(quotient(self.w, 2), 2)
        self.c = rest(self.w, 2)
        self.y = quotient(self.n, 2)
        self.xl = rest(self.n, 2)
        self.x = self.xh * 2 + self.xl
        self.mid = rest(self.xh + self.xl, 2)

    @staticmethod
    def device(z, xh, c, y, xl):
        return (z * 4 + xh * 2 + c, y * 2 + xl)

    def is_me(self, device):
        return both(device[0] == self.w, device[1] == self.n)

    def across(self, a):
        return self.x + (1 - self.mid) * a * (3 - 2 * self.x)

    def step(self, i):
        pair, half = quotient(i, 2), rest(i, 2)
        return quotient(pair, 2) + 2 * half, rest(pair + half, 2)

    def side(self, e):
        return 1 - e + (1 - self.xh) * self.xl * (2 * e - 1)

    def first_leg(self, i):
        d, e = self.step(i)
        a = self.side(e)
        z2 = rest(self.z + self.y + d, 4)
        xr = self.across(a)
        xh2 = self.mid * a + (1 - self.mid) * quotient(xr, 2)
        return z2 * 2 + xh2, self.device(z2, quotient(xr, 2), self.c, self.y, rest(xr, 2))

    def second_leg(self, i, c2):
        d, e = self.step(i)
        a = self.side(e)
        zs = rest(self.z + 8 - self.y - d, 4)
        xs = self.across(a)
        xh2 = self.mid * a + (1 - self.mid) * self.xh
        brick = self.device(self.z, xh2, c2, zs, quotient(xs, 2))
        return brick, self.c * 8 + self.y * 2 + rest(xs, 2)


def coeffs(labels, index, table):
    return [table[index[labels[level]]] for level in range(4)]


def depth_change(field):
    lane = lax.broadcasted_iota(jnp.int32, field.shape, field.ndim - 1)
    up = jnp.where(lane == 127, 0.0, pltpu.roll(field, 127, field.ndim - 1))
    down = jnp.where(lane == 0, 0.0, pltpu.roll(field, 1, field.ndim - 1))
    return up - down


def cross(p, q):
    return (p[1] * q[2] - p[2] * q[1], p[2] * q[0] - p[0] * q[2], p[0] * q[1] - p[1] * q[0])


def forces_kernel(
    grav_levels,
    grav_step,
    seis_levels,
    seis_step,
    labels_in,
    dens_index_in,
    vel_index_in,
    dens_table_in,
    vel_table_in,
    dens_out,
    vel_out,
    grav_slope,
    seis_slope,
    labels,
    dens_index,
    vel_index,
    dens_table,
    vel_table,
    gl,
    gs,
    sl,
    st,
    sb,
    hb,
    rb,
    db,
    xs,
    xr,
    ys,
    yr,
    cs,
    cr,
    grads,
    edge_grads,
    mixes,
    edge_mixes,
    q1e,
    q1s,
    q2s,
    acc,
    df,
    rs,
    rv,
    load_sem,
    leg1_send,
    leg1_recv,
    leg2_send,
    leg2_recv,
    xh_send,
    xh_recv,
    yd_send,
    yd_recv,
    co_send,
    co_recv,
    yv_send,
    yv_recv,
    ret_send,
    ret_recv,
):
    me = Place()
    slab_rows = seis_levels.shape[1]

    barrier = pltpu.get_barrier_semaphore()

    def greet(device):
        pl.semaphore_signal(barrier, inc=1, device_id=device, device_id_type=MESH)

    for dz in range(1, 4):
        greet(me.device((me.z + dz) % 4, me.xh, me.c, me.y, me.xl))

    @pl.when(me.mid == 0)
    def _():
        for z2 in range(4):
            greet(me.device(z2, 1 - me.xh, me.c, me.y, 1 - me.xl))

    for far in range(2):
        x2 = 3 * me.xh if far else 1 + me.xl
        for y2 in range(4):
            for c2 in range(2):
                device = me.device(me.z, x2 // 2, c2, y2, x2 % 2)
                if far:

                    @pl.when(jnp.logical_not(me.is_me(device)))
                    def _():
                        greet(device)

                else:
                    greet(device)

    has_low_x, has_high_x = me.w > 0, me.w < 15
    has_low_y, has_high_y = me.n > 0, me.n < 7
    low_x, high_x = (me.w - 1, me.n), (me.w + 1, me.n)
    low_y, high_y = (me.w, me.n - 1), (me.w, me.n + 1)
    sides = ((has_low_x, low_x), (has_high_x, high_x), (has_low_y, low_y), (has_high_y, high_y))
    corners = [
        (both(sides[sx][0], sides[2 + sy][0]), (me.w + 2 * sx - 1, me.n + 2 * sy - 1))
        for sx in range(2)
        for sy in range(2)
    ]
    for here, device in (*sides, *corners):

        @pl.when(here)
        def _():
            greet(device)

    loads = []
    for number, (source, target) in enumerate(
        [
            (seis_levels, sl.at[:, pl.ds(PAD, slab_rows), :]),
            (labels_in, labels),
            (dens_index_in, dens_index),
            (vel_index_in, vel_index),
            (dens_table_in, dens_table),
            (vel_table_in, vel_table),
            (seis_step, st.at[:, pl.ds(PAD, slab_rows), :]),
            (grav_levels, gl),
            (grav_step, gs),
        ]
    ):
        copy = pltpu.make_async_copy(source, target, load_sem.at[number])
        copy.start()
        loads.append(copy)

    expected = 3 + 4 * (1 - me.mid) + 15 + me.mid
    for here, _ in (*sides, *corners):
        expected = expected + here.astype(jnp.int32)

    for copy in loads[1:6]:
        copy.wait()
    dens_coeff = [0.5 * v for v in coeffs(labels, dens_index, dens_table)]
    vel_coeff = [0.5 * v for v in coeffs(labels, vel_index, vel_table)]

    def remote(source, target, send, recv, device):
        return pltpu.make_async_remote_copy(
            src_ref=source,
            dst_ref=target,
            send_sem=send,
            recv_sem=recv,
            device_id=device,
            device_id_type=MESH,
        )

    def start_any(source, target, send, recv, device):
        mine = me.is_me(device)

        @pl.when(mine)
        def _():
            pltpu.make_async_copy(source, target, recv).start()

        @pl.when(jnp.logical_not(mine))
        def _():
            remote(source, target, send, recv, device).start()

    def await_bytes(ref, sem):
        pltpu.make_async_copy(ref, ref, sem).wait()

    def brick_slot(field, slot):
        return rb.at[field, pl.ds(pl.multiple_of((slot + 1) * MSG, 8), MSG), :]

    def send_slabs(field):
        def one(i, _):
            send_slab(field, i)
            return 0

        lax.fori_loop(0, 8, one, 0)

    def send_slab(field, i):
        pair, relay = me.first_leg(i)
        for c2 in range(2):
            block = pair * 2 + c2
            x_at = block * NX - 2 + lax.broadcasted_iota(jnp.int32, (PITCH, 128), 0)
            inside = both(x_at >= 0, x_at < slab_rows // 2)
            for column in range(2):
                rows = pl.ds(block * 2 * NX + PAD - 4 + column, PITCH, stride=2)
                total = None
                for level in range(4):
                    t = jnp.tanh(sl[level, rows, :])
                    if field == 0:
                        term = vel_coeff[level] * (1.0 + t)
                    else:
                        term = (vel_coeff[level] * (1.0 - t * t)) * st[level, rows, :]
                    total = term if total is None else total + term
                sb[field, i, pl.ds((c2 * 2 + column) * PITCH, PITCH), :] = jnp.where(
                    inside, total, 0.0
                )
        mine = me.is_me(relay)

        @pl.when(mine)
        def _():
            second_leg(field, i, sb)

        @pl.when(jnp.logical_not(mine))
        def _():
            remote(
                sb.at[field, i], hb.at[field, i], leg1_send.at[field], leg1_recv.at[field, i], relay
            ).start()

    def relay_slab(field, i):
        @pl.when(jnp.logical_not(me.is_me(me.first_leg(i)[1])))
        def _():
            await_bytes(hb.at[field, i], leg1_recv.at[field, i])
            second_leg(field, i, hb)

    def second_leg(field, i, held):
        for c2 in range(2):
            brick, slot = me.second_leg(i, c2)
            which = (slot > 0).astype(jnp.int32) + (slot > 14).astype(jnp.int32)
            start_any(
                held.at[field, i, pl.ds(c2 * MSG, MSG), :],
                brick_slot(field, slot),
                leg2_send.at[field],
                leg2_recv.at[field, which],
                brick,
            )

    loads[0].wait()
    pl.semaphore_wait(barrier, expected)
    send_slabs(0)

    loads[7].wait()
    loads[8].wait()

    def dens_row(x):
        dens, change = None, None
        for level in range(4):
            t = jnp.tanh(gl[level, x])
            term = dens_coeff[level] * (1.0 + t)
            slope = dens_coeff[level] * (1.0 - t * t)
            grav_slope[level, x] = slope * (1.0 / 16.0)
            slope = slope * gs[level, x]
            dens = term if dens is None else dens + term
            change = slope if change is None else change + slope
        rows = pl.ds(2 * PITCH + 2 + x, NY, stride=PITCH)
        db[0, rows, :] = dens
        db[1, rows, :] = change
        return dens, change

    def edge_row(k, _):
        side, row = k // 2, k % 2
        dens, change = dens_row(side * (NX - 2) + row)
        xs[side, pl.ds(pl.multiple_of(row * NY, 8), NY), :] = dens
        xs[side, pl.ds(pl.multiple_of((2 + row) * NY, 8), NY), :] = change
        return 0

    lax.fori_loop(0, 4, edge_row, 0)

    def x_halo(side):
        return remote(
            xs.at[side],
            xr.at[1 - side],
            xh_send.at[side],
            xh_recv.at[1 - side],
            (low_x, high_x)[side],
        )

    for side in range(2):

        @pl.when(sides[side][0])
        def _():
            x_halo(side).start()

    def inner_row(x, _):
        dens_row(x)
        return 0

    lax.fori_loop(2, NX - 2, inner_row, 0)

    for side in range(2):
        for field in range(2):
            for column in range(2):
                ys[side, pl.ds((field * 2 + column) * NX, NX), :] = db[
                    field, pl.ds((2 + side * (NY - 2) + column) * PITCH + 2, NX), :
                ]
    cs[...] = jnp.zeros(cs.shape, jnp.float32)
    for k in range(4):
        at = (2 + k % 2 * (NY - 1)) * PITCH + 2 + k // 2 * (NX - 1)
        for field in range(2):
            cs[k, pl.ds(field, 1), :] = db[field, pl.ds(at, 1), :]

    def y_side(side):
        return remote(
            ys.at[side], yr.at[1 - side], yd_send.at[side], yd_recv.at[1 - side], sides[2 + side][1]
        )

    def corner(k):
        return remote(cs.at[k], cr.at[3 - k], co_send.at[k], co_recv.at[3 - k], corners[k][1])

    dens_halos = [
        *((sides[side][0], x_halo(side), xr.at[side], xh_recv.at[side]) for side in range(2)),
        *((sides[2 + side][0], y_side(side), yr.at[side], yd_recv.at[side]) for side in range(2)),
        *((corners[k][0], corner(k), cr.at[k], co_recv.at[k]) for k in range(4)),
    ]
    for here, copy, _, _ in dens_halos[2:]:

        @pl.when(here)
        def _():
            copy.start()

    loads[6].wait()

    def relay_and_send(i):
        relay_slab(0, i)
        send_slab(1, i)

    for i in range(8):
        relay_and_send(i)

    def y_halo(field, side):
        source = rb.at[field, pl.ds((2 + side * (NY - 2)) * PITCH, MSG), :]
        target = rb.at[field, pl.ds((1 - side) * (NY + 2) * PITCH, MSG), :]
        return remote(
            source, target, yv_send.at[field, side], yv_recv.at[field, 1 - side], (low_y, high_y)[side]
        )

    def y_halo_start(field):
        for side in range(2):

            @pl.when(sides[2 + side][0])
            def _():
                y_halo(field, side).start()

            @pl.when(jnp.logical_not(sides[2 + side][0]))
            def _():
                rb[field, pl.ds(side * (NY + 2) * PITCH, MSG), :] = jnp.zeros(
                    (MSG, 128), jnp.float32
                )

    def y_halo_recv(field):
        for side in range(2):

            @pl.when(sides[2 + side][0])
            def _():
                await_bytes(
                    rb.at[field, pl.ds(side * (NY + 2) * PITCH, MSG), :], yv_recv.at[field, side]
                )

    def y_halo_sent(field):
        for side in range(2):

            @pl.when(sides[2 + side][0])
            def _():
                y_halo(field, side).wait_send()

    def y_halo_early(field):
        for slot in (0, 15):
            await_bytes(brick_slot(field, slot), leg2_recv.at[field, slot // 15 * 2])
        y_halo_start(field)

    def relay_second(i):
        relay_slab(1, i)

    for i in range(8):
        relay_second(i)
    y_halo_early(0)

    for here, _, ref, recv in dens_halos:

        @pl.when(here)
        def _():
            await_bytes(ref, recv)

        @pl.when(jnp.logical_not(here))
        def _():
            ref[...] = jnp.zeros(ref.shape, jnp.float32)

    for field in range(2):
        for side in range(2):
            for row in range(2):
                db[field, pl.ds(2 * PITCH + side * (NX + 2) + row, NY, stride=PITCH), :] = xr[
                    side, pl.ds((field * 2 + row) * NY, NY), :
                ]
                db[field, pl.ds((side * (NY + 2) + row) * PITCH + 2, NX), :] = yr[
                    side, pl.ds((field * 2 + row) * NX, NX), :
                ]
        for k in range(4):
            at = (1 + k % 2 * (NY + 1)) * PITCH + 1 + k // 2 * (NX + 1)
            db[field, pl.ds(at, 1), :] = cr[k, pl.ds(field, 1), :]

    def gradient(ref, field, yy):
        def at(column, x):
            return ref[field, pl.ds(column * PITCH + 2 + x, NX), :]

        return (
            at(yy, 1) - at(yy, -1),
            at(yy + 1, 0) - at(yy - 1, 0),
            depth_change(at(yy, 0)),
        )

    def edge_gradient(ref, field, side, rows):
        x = (-1, NX)[side]

        def at(dy, x):
            start = (rows.start + 2 + dy) * PITCH + 2 + x
            return ref[field, pl.ds(start, rows.size, stride=PITCH), :]

        return (at(0, x + 1) - at(0, x - 1), at(1, x) - at(-1, x), depth_change(at(0, x)))

    every, inner_rows = pl.ds(0, NY), pl.ds(1, NY - 2)

    def keep(ref, *at_and_vector):
        *at, vector = at_and_vector
        for number in range(3):
            ref[(at[0], number, *at[1:])] = vector[number]

    def kept(ref, *at):
        return tuple(ref[(at[0], number, *at[1:])] for number in range(3))

    def columns(body, first, count, batch):
        def some(j, _):
            body([first + j * batch + k for k in range(batch)])
            return 0

        lax.fori_loop(0, count // batch, some, 0)

    def dens_gradient(field):
        def some(yys):
            for yy in yys:
                keep(grads, field, yy, gradient(db, field, yy))

        columns(some, 2, NY, 4)
        some([1, NY + 2])
        for side in range(2):
            keep(edge_grads, field, side, every, edge_gradient(db, field, side, every))

    def mixed(field, own, grads, *at):
        first = cross(kept(grads, 0, *at), own)
        if field == 0:
            return first
        second = cross(kept(grads, 1, *at), kept(grads, 2, *at))
        return tuple(s + t for s, t in zip(second, first))

    def masked(vector, inside):
        factor = inside.astype(jnp.float32)
        return tuple(v * factor for v in vector)

    def vel_columns(field, yys, inside=None):
        qs = []
        for number, yy in enumerate(yys):
            own = gradient(rb, field, yy)
            mix = mixed(field, own, grads, yy)
            if inside is not None:
                mix = masked(mix, inside[number])
            keep(grads, 2 + field, yy, own)
            keep(mixes, field, yy, mix)
            qs.append(cross(mix, kept(grads, 0, yy)))
        collect(qs, yys)

    def vel_edges(field, rows):
        for side in range(2):
            own = edge_gradient(rb, field, side, rows)
            mix = masked(mixed(field, own, edge_grads, side, rows), sides[side][0])
            keep(edge_grads, 2 + field, side, rows, own)
            keep(edge_mixes, field, side, rows, mix)
            dens = kept(edge_grads, 0, side, rows)
            q1e[side, rows] = mix[1] * dens[2] - mix[2] * dens[1]

    def dens_columns(field, yys):
        collect([cross(kept(grads, 2, yy), kept(mixes, field, yy)) for yy in yys], yys)

    def dens_edges(field):
        for side in range(2):
            vel, mix = kept(edge_grads, 2, side, every), kept(edge_mixes, field, side, every)
            q1e[side] = vel[1] * mix[2] - vel[2] * mix[1]

    def collect(qs, yys):
        for k, (q, yy) in enumerate(zip(qs, yys)):
            y = jnp.clip(yy - 2, 0, NY - 1)
            q1s[k, pl.ds(8, NX), :] = q[0]
            q1s[k, pl.ds(7, 1), :] = q1e[0, pl.ds(y, 1), :]
            q1s[k, pl.ds(8 + NX, 1), :] = q1e[1, pl.ds(y, 1), :]
            q2s[yy] = q[1]
        turned = [depth_change(q[2]) for q in qs]
        for k, yy in enumerate(yys):
            acc[yy] = q1s[k, pl.ds(7, NX), :] - q1s[k, pl.ds(9, NX), :] - turned[k]

    def adjoint(yy):
        return acc[yy] + (q2s[yy - 1] - q2s[yy + 1])

    def compute(field):
        vel_edges(field, inner_rows)

        columns(lambda yys: vel_columns(field, yys), 3, NY - 2, 5)
        if field == 0:
            y_halo_early(1)
        y_halo_recv(field)
        vel_edges(field, every)
        true = me.n >= 0
        vel_columns(field, [1, 2, NY + 1, NY + 2], [me.n > 0, true, true, me.n < 7])

        def back(i):
            for c2 in range(2):
                p = (i * 2 + c2 + 8 * field) % 16
                slab = (me.n * 2 + p // 8, p % 8)
                for half in range(2):
                    rs[field, p, pl.ds(half * NX, NX), :] = adjoint(2 * p + 2 + half)
                start_any(
                    rs.at[field, p], rv.at[field, me.w], ret_send.at[field], ret_recv.at[field], slab
                )

        for i in range(8):
            back(i)

    def arrive(field):
        await_bytes(rb.at[field, pl.ds(2 * MSG, 14 * MSG), :], leg2_recv.at[field, 1])

    for field in range(2):
        dens_gradient(field)
    arrive(0)
    compute(0)
    arrive(1)
    compute(1)

    for field in range(2):
        dens_edges(field)

        columns(lambda yys: dens_columns(field, yys), 2, NY, 4)
        dens_columns(field, [1, NY + 2])

        def keep_force(y, _):
            for k in range(4):
                at = pl.ds(pl.multiple_of((4 * y + k) * NX, 8), NX)
                df[field, at, :] = adjoint(4 * y + k + 2)
            return 0

        lax.fori_loop(0, NY // 4, keep_force, 0)

    for field in range(2):

        def turn(x, _):
            dens_out[field, x] = df[field, pl.ds(x, NY, stride=NX), :]
            return 0

        lax.fori_loop(0, NX, turn, 0)

    def seis_rows(i, _):
        for level in range(4):
            t = jnp.tanh(sl[level, pl.ds(pl.multiple_of(PAD + i * 32, 8), 32), :])
            scale = vel_coeff[level] * (1.0 / 16.0)
            seis_slope[level, pl.ds(pl.multiple_of(i * 32, 8), 32), :] = scale * (1.0 - t * t)
        return 0

    lax.fori_loop(0, slab_rows // 32, seis_rows, 0)

    for field in range(2):

        await_bytes(rv.at[field], ret_recv.at[field])

        def finish(block, _):
            for half in range(2):
                vel_out[field, pl.ds(block * 2 * NX + half, NX, stride=2), :] = rv[
                    field, block, pl.ds(half * NX, NX), :
                ]
            return 0

        lax.fori_loop(0, 16, finish, 0)

    for here, copy, _, _ in dens_halos:

        @pl.when(here)
        def _():
            copy.wait_send()

    for field in range(2):
        y_halo_sent(field)

        await_bytes(sb.at[field, pl.ds(0, 6)], leg1_send.at[field])
        await_bytes(rb.at[field, pl.ds(0, 15 * MSG), :], leg2_send.at[field])
        await_bytes(rs.at[field, pl.ds(0, 15)], ret_send.at[field])

        @pl.when(me.mid == 0)
        def _():
            await_bytes(sb.at[field, 0], leg1_send.at[field])

        @pl.when(me.mid == 1)
        def _():
            await_bytes(rb.at[field, pl.ds(0, MSG), :], leg2_send.at[field])

        @pl.when(me.w // 2 != me.n)
        def _():
            await_bytes(rs.at[field, 0], ret_send.at[field])


def chain_kernel(
    steps,
    dens_force,
    vel_force,
    grav_slope,
    seis_slope,
    grav_gradient,
    grav_curvature,
    seis_gradient,
    seis_curvature,
    brick_outs,
    slab_outs,
    sems,
):
    parts = (
        (grav_slope, dens_force, (grav_gradient, grav_curvature), brick_outs, 0),
        (seis_slope, vel_force, (seis_gradient, seis_curvature), slab_outs, 2),
    )

    def step(i, _):
        for slope, force, outs, made, sem in parts:
            rows = slope.shape[1] // steps
            here = pl.ds(i * rows, rows)
            for level in range(4):
                factor = slope[level, here]
                for number in range(2):
                    made[number, level, here] = factor * force[number, here]
            for number in range(2):
                pltpu.make_async_copy(
                    made.at[number, :, here], outs[number].at[:, here], sems.at[sem + number]
                ).start()
        return 0

    lax.fori_loop(0, steps, step, 0)
    for _, _, outs, made, sem in parts:
        for number in range(2):
            pltpu.make_async_copy(made.at[number], outs[number], sems.at[sem + number]).wait()


def shards(
    grav_levels,
    grav_step,
    seis_levels,
    seis_step,
    unit_labels,
    dens_index,
    vel_index,
    dens_table,
    vel_table,
):
    levels, nx, ny, nz = grav_levels.shape
    slab_x, slab_y = seis_levels.shape[1:3]
    rows = slab_x * slab_y
    seis_rows = seis_levels.reshape(levels, rows, nz)
    step_rows = seis_step.reshape(levels, rows, nz)
    tables = (unit_labels, dens_index, vel_index, dens_table, vel_table)
    hbm = pl.BlockSpec(memory_space=pltpu.HBM)
    vmem = pl.BlockSpec(memory_space=pltpu.VMEM)
    f32 = jnp.float32
    dma = pltpu.SemaphoreType.DMA
    brick_shape = jax.ShapeDtypeStruct(grav_levels.shape, f32)
    slab_shape = jax.ShapeDtypeStruct(seis_rows.shape, f32)
    forces = pl.pallas_call(
        forces_kernel,
        out_shape=(
            jax.ShapeDtypeStruct((2, nx, ny, nz), f32),
            jax.ShapeDtypeStruct((2, rows, nz), f32),
            brick_shape,
            slab_shape,
        ),
        in_specs=[hbm] * 9,
        out_specs=(vmem,) * 4,
        scratch_shapes=[
            *(pltpu.SMEM(table.shape, table.dtype) for table in tables),
            pltpu.VMEM((levels, nx, ny, nz), f32),
            pltpu.VMEM((levels, nx, ny, nz), f32),
            pltpu.VMEM((levels, rows + 4 * PAD, nz), f32),
            pltpu.VMEM((levels, rows + 4 * PAD, nz), f32),
            pltpu.VMEM((2, 8, 2 * MSG, nz), f32),
            pltpu.VMEM((2, 8, 2 * MSG, nz), f32),
            pltpu.VMEM((2, COLS, nz), f32),
            pltpu.VMEM((2, COLS, nz), f32),
            pltpu.VMEM((2, 4 * NY, nz), f32),
            pltpu.VMEM((2, 4 * NY, nz), f32),
            pltpu.VMEM((2, 4 * NX, nz), f32),
            pltpu.VMEM((2, 4 * NX, nz), f32),
            pltpu.VMEM((4, 8, nz), f32),
            pltpu.VMEM((4, 8, nz), f32),
            pltpu.VMEM((4, 3, NY + 4, NX, nz), f32),
            pltpu.VMEM((4, 3, 2, NY, nz), f32),
            pltpu.VMEM((2, 3, NY + 4, NX, nz), f32),
            pltpu.VMEM((2, 3, 2, NY, nz), f32),
            pltpu.VMEM((2, NY, nz), f32),
            pltpu.VMEM((5, NX + 16, nz), f32),
            pltpu.VMEM((NY + 4, NX, nz), f32),
            pltpu.VMEM((NY + 4, NX, nz), f32),
            pltpu.VMEM((2, NY * NX, nz), f32),
            pltpu.VMEM((2, 16, 2 * NX, nz), f32),
            pltpu.VMEM((2, 16, 2 * NX, nz), f32),
            dma((9,)),
            dma((2,)),
            dma((2, 8)),
            dma((2,)),
            dma((2, 3)),
            dma((2,)),
            dma((2,)),
            dma((2,)),
            dma((2,)),
            dma((4,)),
            dma((4,)),
            dma((2, 2)),
            dma((2, 2)),
            dma((2,)),
            dma((2,)),
        ],
        compiler_params=pltpu.CompilerParams(
            collective_id=0, has_side_effects=True, vmem_limit_bytes=42 << 20
        ),
        name="forces",
    )(*(pltpu.with_memory_space_constraint(v, pltpu.HBM) for v in (grav_levels, grav_step, seis_rows, step_rows, *tables)))

    outs = pl.pallas_call(
        functools.partial(chain_kernel, 8),
        out_shape=(brick_shape, brick_shape, slab_shape, slab_shape),
        in_specs=[vmem] * 4,
        out_specs=(hbm,) * 4,
        scratch_shapes=[
            pltpu.VMEM((2, *brick_shape.shape), f32),
            pltpu.VMEM((2, *slab_shape.shape), f32),
            dma((4,)),
        ],
        compiler_params=pltpu.CompilerParams(vmem_limit_bytes=32 << 20),
        name="chain",
    )(*forces)
    return (
        outs[0],
        outs[1],
        outs[2].reshape(seis_levels.shape),
        outs[3].reshape(seis_levels.shape),
    )


def solution(mesh):
    placed = (
        P(None, "wide", "narrow", None),
        P(None, "wide", "narrow", None),
        P(None, None, ("wide", "narrow"), None),
        P(None, None, ("wide", "narrow"), None),
        P(),
        P(),
        P(),
        P(),
        P(),
    )
    return jax.shard_map(
        shards,
        mesh=mesh,
        in_specs=placed,
        out_specs=placed[:4],
        check_vma=False,
    )
```

```python
import functools

import jax
import jax.numpy as jnp
from jax import lax
from jax.experimental import pallas as pl
from jax.experimental.pallas import tpu as pltpu
from jax.sharding import PartitionSpec as P

MESH = pl.DeviceIdType.MESH
NX = 32
NY = 32
PITCH = NX + 4
MSG = 2 * PITCH
COLS = (NY + 4) * PITCH
PAD = 8


def quotient(value, by):
    return value // by if isinstance(value, int) else lax.div(value, jnp.int32(by))


def rest(value, by):
    return value % by if isinstance(value, int) else lax.rem(value, jnp.int32(by))


def both(one, other):
    return jnp.logical_and(one, other)


class Place:
    def __init__(self):
        self.w = lax.axis_index("wide")
        self.n = lax.axis_index("narrow")
        self.z = quotient(self.w, 4)
        self.xh = rest(quotient(self.w, 2), 2)
        self.c = rest(self.w, 2)
        self.y = quotient(self.n, 2)
        self.xl = rest(self.n, 2)
        self.x = self.xh * 2 + self.xl
        self.mid = rest(self.xh + self.xl, 2)

    @staticmethod
    def device(z, xh, c, y, xl):
        return (z * 4 + xh * 2 + c, y * 2 + xl)

    def is_me(self, device):
        return both(device[0] == self.w, device[1] == self.n)

    def across(self, a):
        return self.x + (1 - self.mid) * a * (3 - 2 * self.x)

    def step(self, i):
        pair, half = quotient(i, 2), rest(i, 2)
        return quotient(pair, 2) + 2 * half, rest(pair + half, 2)

    def side(self, e):
        return 1 - e + (1 - self.xh) * self.xl * (2 * e - 1)

    def first_leg(self, i):
        d, e = self.step(i)
        a = self.side(e)
        z2 = rest(self.z + self.y + d, 4)
        xr = self.across(a)
        xh2 = self.mid * a + (1 - self.mid) * quotient(xr, 2)
        return z2 * 2 + xh2, self.device(z2, quotient(xr, 2), self.c, self.y, rest(xr, 2))

    def second_leg(self, i, c2):
        d, e = self.step(i)
        a = self.side(e)
        zs = rest(self.z + 8 - self.y - d, 4)
        xs = self.across(a)
        xh2 = self.mid * a + (1 - self.mid) * self.xh
        brick = self.device(self.z, xh2, c2, zs, quotient(xs, 2))
        return brick, self.c * 8 + self.y * 2 + rest(xs, 2)


def coeffs(labels, index, table):
    return [table[index[labels[level]]] for level in range(4)]


def depth_change(field):
    lane = lax.broadcasted_iota(jnp.int32, field.shape, field.ndim - 1)
    up = jnp.where(lane == 127, 0.0, pltpu.roll(field, 127, field.ndim - 1))
    down = jnp.where(lane == 0, 0.0, pltpu.roll(field, 1, field.ndim - 1))
    return up - down


def cross(p, q):
    return (p[1] * q[2] - p[2] * q[1], p[2] * q[0] - p[0] * q[2], p[0] * q[1] - p[1] * q[0])


def forces_kernel(
    grav_levels,
    grav_step,
    seis_levels,
    seis_step,
    labels_in,
    dens_index_in,
    vel_index_in,
    dens_table_in,
    vel_table_in,
    dens_out,
    vel_out,
    grav_slope,
    seis_slope,
    labels,
    dens_index,
    vel_index,
    dens_table,
    vel_table,
    gl,
    gs,
    sl,
    st,
    sb,
    hb,
    rb,
    db,
    xs,
    xr,
    ys,
    yr,
    cs,
    cr,
    grads,
    edge_grads,
    mixes,
    edge_mixes,
    q1e,
    q1s,
    q2s,
    acc,
    df,
    rs,
    rv,
    load_sem,
    leg1_send,
    leg1_recv,
    leg2_send,
    leg2_recv,
    xh_send,
    xh_recv,
    yd_send,
    yd_recv,
    co_send,
    co_recv,
    yv_send,
    yv_recv,
    ret_send,
    ret_recv,
):
    me = Place()
    slab_rows = seis_levels.shape[1]

    barrier = pltpu.get_barrier_semaphore()

    def greet(device):
        pl.semaphore_signal(barrier, inc=1, device_id=device, device_id_type=MESH)

    for dz in range(1, 4):
        greet(me.device((me.z + dz) % 4, me.xh, me.c, me.y, me.xl))

    @pl.when(me.mid == 0)
    def _():
        for z2 in range(4):
            greet(me.device(z2, 1 - me.xh, me.c, me.y, 1 - me.xl))

    for far in range(2):
        x2 = 3 * me.xh if far else 1 + me.xl
        for y2 in range(4):
            for c2 in range(2):
                device = me.device(me.z, x2 // 2, c2, y2, x2 % 2)
                if far:

                    @pl.when(jnp.logical_not(me.is_me(device)))
                    def _():
                        greet(device)

                else:
                    greet(device)

    has_low_x, has_high_x = me.w > 0, me.w < 15
    has_low_y, has_high_y = me.n > 0, me.n < 7
    low_x, high_x = (me.w - 1, me.n), (me.w + 1, me.n)
    low_y, high_y = (me.w, me.n - 1), (me.w, me.n + 1)
    sides = ((has_low_x, low_x), (has_high_x, high_x), (has_low_y, low_y), (has_high_y, high_y))
    corners = [
        (both(sides[sx][0], sides[2 + sy][0]), (me.w + 2 * sx - 1, me.n + 2 * sy - 1))
        for sx in range(2)
        for sy in range(2)
    ]
    for here, device in (*sides, *corners):

        @pl.when(here)
        def _():
            greet(device)

    loads = []
    for number, (source, target) in enumerate(
        [
            (seis_levels, sl.at[:, pl.ds(PAD, slab_rows), :]),
            (labels_in, labels),
            (dens_index_in, dens_index),
            (vel_index_in, vel_index),
            (dens_table_in, dens_table),
            (vel_table_in, vel_table),
            (seis_step, st.at[:, pl.ds(PAD, slab_rows), :]),
            (grav_levels, gl),
            (grav_step, gs),
        ]
    ):
        copy = pltpu.make_async_copy(source, target, load_sem.at[number])
        copy.start()
        loads.append(copy)

    expected = 3 + 4 * (1 - me.mid) + 15 + me.mid
    for here, _ in (*sides, *corners):
        expected = expected + here.astype(jnp.int32)

    for copy in loads[1:6]:
        copy.wait()
    dens_coeff = [0.5 * v for v in coeffs(labels, dens_index, dens_table)]
    vel_coeff = [0.5 * v for v in coeffs(labels, vel_index, vel_table)]

    def remote(source, target, send, recv, device):
        return pltpu.make_async_remote_copy(
            src_ref=source,
            dst_ref=target,
            send_sem=send,
            recv_sem=recv,
            device_id=device,
            device_id_type=MESH,
        )

    def start_any(source, target, send, recv, device):
        mine = me.is_me(device)

        @pl.when(mine)
        def _():
            pltpu.make_async_copy(source, target, recv).start()

        @pl.when(jnp.logical_not(mine))
        def _():
            remote(source, target, send, recv, device).start()

    def await_bytes(ref, sem):
        pltpu.make_async_copy(ref, ref, sem).wait()

    def brick_slot(field, slot):
        return rb.at[field, pl.ds(pl.multiple_of((slot + 1) * MSG, 8), MSG), :]

    def send_slabs(field):
        def one(i, _):
            send_slab(field, i)
            return 0

        lax.fori_loop(0, 8, one, 0)

    def send_slab(field, i):
        pair, relay = me.first_leg(i)
        for c2 in range(2):
            block = pair * 2 + c2
            x_at = block * NX - 2 + lax.broadcasted_iota(jnp.int32, (PITCH, 128), 0)
            inside = both(x_at >= 0, x_at < slab_rows // 2)
            for column in range(2):
                rows = pl.ds(block * 2 * NX + PAD - 4 + column, PITCH, stride=2)
                total = None
                for level in range(4):
                    t = jnp.tanh(sl[level, rows, :])
                    if field == 0:
                        term = vel_coeff[level] * (1.0 + t)
                    else:
                        term = (vel_coeff[level] * (1.0 - t * t)) * st[level, rows, :]
                    total = term if total is None else total + term
                sb[field, i, pl.ds((c2 * 2 + column) * PITCH, PITCH), :] = jnp.where(
                    inside, total, 0.0
                )
        mine = me.is_me(relay)

        @pl.when(mine)
        def _():
            second_leg(field, i, sb)

        @pl.when(jnp.logical_not(mine))
        def _():
            remote(
                sb.at[field, i], hb.at[field, i], leg1_send.at[field], leg1_recv.at[field, i], relay
            ).start()

    def relay_slab(field, i):
        @pl.when(jnp.logical_not(me.is_me(me.first_leg(i)[1])))
        def _():
            await_bytes(hb.at[field, i], leg1_recv.at[field, i])
            second_leg(field, i, hb)

    def second_leg(field, i, held):
        for c2 in range(2):
            brick, slot = me.second_leg(i, c2)
            which = (slot > 0).astype(jnp.int32) + (slot > 14).astype(jnp.int32)
            start_any(
                held.at[field, i, pl.ds(c2 * MSG, MSG), :],
                brick_slot(field, slot),
                leg2_send.at[field],
                leg2_recv.at[field, which],
                brick,
            )

    loads[0].wait()
    pl.semaphore_wait(barrier, expected)
    send_slabs(0)

    loads[7].wait()
    loads[8].wait()

    def dens_row(x):
        dens, change = None, None
        for level in range(4):
            t = jnp.tanh(gl[level, x])
            term = dens_coeff[level] * (1.0 + t)
            slope = dens_coeff[level] * (1.0 - t * t)
            grav_slope[level, x] = slope * (1.0 / 16.0)
            slope = slope * gs[level, x]
            dens = term if dens is None else dens + term
            change = slope if change is None else change + slope
        rows = pl.ds(2 * PITCH + 2 + x, NY, stride=PITCH)
        db[0, rows, :] = dens
        db[1, rows, :] = change
        return dens, change

    def edge_row(k, _):
        side, row = k // 2, k % 2
        dens, change = dens_row(side * (NX - 2) + row)
        xs[side, pl.ds(pl.multiple_of(row * NY, 8), NY), :] = dens
        xs[side, pl.ds(pl.multiple_of((2 + row) * NY, 8), NY), :] = change
        return 0

    lax.fori_loop(0, 4, edge_row, 0)

    def x_halo(side):
        return remote(
            xs.at[side],
            xr.at[1 - side],
            xh_send.at[side],
            xh_recv.at[1 - side],
            (low_x, high_x)[side],
        )

    for side in range(2):

        @pl.when(sides[side][0])
        def _():
            x_halo(side).start()

    def inner_row(x, _):
        dens_row(x)
        return 0

    lax.fori_loop(2, NX - 2, inner_row, 0)

    for side in range(2):
        for field in range(2):
            for column in range(2):
                ys[side, pl.ds((field * 2 + column) * NX, NX), :] = db[
                    field, pl.ds((2 + side * (NY - 2) + column) * PITCH + 2, NX), :
                ]
    cs[...] = jnp.zeros(cs.shape, jnp.float32)
    for k in range(4):
        at = (2 + k % 2 * (NY - 1)) * PITCH + 2 + k // 2 * (NX - 1)
        for field in range(2):
            cs[k, pl.ds(field, 1), :] = db[field, pl.ds(at, 1), :]

    def y_side(side):
        return remote(
            ys.at[side], yr.at[1 - side], yd_send.at[side], yd_recv.at[1 - side], sides[2 + side][1]
        )

    def corner(k):
        return remote(cs.at[k], cr.at[3 - k], co_send.at[k], co_recv.at[3 - k], corners[k][1])

    dens_halos = [
        *((sides[side][0], x_halo(side), xr.at[side], xh_recv.at[side]) for side in range(2)),
        *((sides[2 + side][0], y_side(side), yr.at[side], yd_recv.at[side]) for side in range(2)),
        *((corners[k][0], corner(k), cr.at[k], co_recv.at[k]) for k in range(4)),
    ]
    for here, copy, _, _ in dens_halos[2:]:

        @pl.when(here)
        def _():
            copy.start()

    loads[6].wait()

    def relay_and_send(i):
        relay_slab(0, i)
        send_slab(1, i)

    for i in range(8):
        relay_and_send(i)

    def y_halo(field, side):
        source = rb.at[field, pl.ds((2 + side * (NY - 2)) * PITCH, MSG), :]
        target = rb.at[field, pl.ds((1 - side) * (NY + 2) * PITCH, MSG), :]
        return remote(
            source, target, yv_send.at[field, side], yv_recv.at[field, 1 - side], (low_y, high_y)[side]
        )

    def y_halo_start(field):
        for side in range(2):

            @pl.when(sides[2 + side][0])
            def _():
                y_halo(field, side).start()

            @pl.when(jnp.logical_not(sides[2 + side][0]))
            def _():
                rb[field, pl.ds(side * (NY + 2) * PITCH, MSG), :] = jnp.zeros(
                    (MSG, 128), jnp.float32
                )

    def y_halo_recv(field):
        for side in range(2):

            @pl.when(sides[2 + side][0])
            def _():
                await_bytes(
                    rb.at[field, pl.ds(side * (NY + 2) * PITCH, MSG), :], yv_recv.at[field, side]
                )

    def y_halo_sent(field):
        for side in range(2):

            @pl.when(sides[2 + side][0])
            def _():
                y_halo(field, side).wait_send()

    def y_halo_early(field):
        for slot in (0, 15):
            await_bytes(brick_slot(field, slot), leg2_recv.at[field, slot // 15 * 2])
        y_halo_start(field)

    def relay_second(i):
        relay_slab(1, i)

    for i in range(8):
        relay_second(i)
    y_halo_early(0)

    for here, _, ref, recv in dens_halos:

        @pl.when(here)
        def _():
            await_bytes(ref, recv)

        @pl.when(jnp.logical_not(here))
        def _():
            ref[...] = jnp.zeros(ref.shape, jnp.float32)

    for field in range(2):
        for side in range(2):
            for row in range(2):
                db[field, pl.ds(2 * PITCH + side * (NX + 2) + row, NY, stride=PITCH), :] = xr[
                    side, pl.ds((field * 2 + row) * NY, NY), :
                ]
                db[field, pl.ds((side * (NY + 2) + row) * PITCH + 2, NX), :] = yr[
                    side, pl.ds((field * 2 + row) * NX, NX), :
                ]
        for k in range(4):
            at = (1 + k % 2 * (NY + 1)) * PITCH + 1 + k // 2 * (NX + 1)
            db[field, pl.ds(at, 1), :] = cr[k, pl.ds(field, 1), :]

    def gradient(ref, field, yy):
        def at(column, x):
            return ref[field, pl.ds(column * PITCH + 2 + x, NX), :]

        return (
            at(yy, 1) - at(yy, -1),
            at(yy + 1, 0) - at(yy - 1, 0),
            depth_change(at(yy, 0)),
        )

    def edge_gradient(ref, field, side, rows):
        x = (-1, NX)[side]

        def at(dy, x):
            start = (rows.start + 2 + dy) * PITCH + 2 + x
            return ref[field, pl.ds(start, rows.size, stride=PITCH), :]

        return (at(0, x + 1) - at(0, x - 1), at(1, x) - at(-1, x), depth_change(at(0, x)))

    every, inner_rows = pl.ds(0, NY), pl.ds(1, NY - 2)

    def keep(ref, *at_and_vector):
        *at, vector = at_and_vector
        for number in range(3):
            ref[(at[0], number, *at[1:])] = vector[number]

    def kept(ref, *at):
        return tuple(ref[(at[0], number, *at[1:])] for number in range(3))

    def columns(body, first, count, batch):
        def some(j, _):
            body([first + j * batch + k for k in range(batch)])
            return 0

        lax.fori_loop(0, count // batch, some, 0)

    def dens_gradient(field):
        def some(yys):
            for yy in yys:
                keep(grads, field, yy, gradient(db, field, yy))

        columns(some, 2, NY, 4)
        some([1, NY + 2])
        for side in range(2):
            keep(edge_grads, field, side, every, edge_gradient(db, field, side, every))

    def mixed(field, own, grads, *at):
        first = cross(kept(grads, 0, *at), own)
        if field == 0:
            return first
        second = cross(kept(grads, 1, *at), kept(grads, 2, *at))
        return tuple(s + t for s, t in zip(second, first))

    def masked(vector, inside):
        factor = inside.astype(jnp.float32)
        return tuple(v * factor for v in vector)

    def vel_columns(field, yys, inside=None):
        qs = []
        for number, yy in enumerate(yys):
            own = gradient(rb, field, yy)
            mix = mixed(field, own, grads, yy)
            if inside is not None:
                mix = masked(mix, inside[number])
            keep(grads, 2 + field, yy, own)
            keep(mixes, field, yy, mix)
            qs.append(cross(mix, kept(grads, 0, yy)))
        collect(qs, yys)

    def vel_edges(field, rows):
        for side in range(2):
            own = edge_gradient(rb, field, side, rows)
            mix = masked(mixed(field, own, edge_grads, side, rows), sides[side][0])
            keep(edge_grads, 2 + field, side, rows, own)
            keep(edge_mixes, field, side, rows, mix)
            dens = kept(edge_grads, 0, side, rows)
            q1e[side, rows] = mix[1] * dens[2] - mix[2] * dens[1]

    def dens_columns(field, yys):
        collect([cross(kept(grads, 2, yy), kept(mixes, field, yy)) for yy in yys], yys)

    def dens_edges(field):
        for side in range(2):
            vel, mix = kept(edge_grads, 2, side, every), kept(edge_mixes, field, side, every)
            q1e[side] = vel[1] * mix[2] - vel[2] * mix[1]

    def collect(qs, yys):
        for k, (q, yy) in enumerate(zip(qs, yys)):
            y = jnp.clip(yy - 2, 0, NY - 1)
            q1s[k, pl.ds(8, NX), :] = q[0]
            q1s[k, pl.ds(7, 1), :] = q1e[0, pl.ds(y, 1), :]
            q1s[k, pl.ds(8 + NX, 1), :] = q1e[1, pl.ds(y, 1), :]
            q2s[yy] = q[1]
        turned = [depth_change(q[2]) for q in qs]
        for k, yy in enumerate(yys):
            acc[yy] = q1s[k, pl.ds(7, NX), :] - q1s[k, pl.ds(9, NX), :] - turned[k]

    def adjoint(yy):
        return acc[yy] + (q2s[yy - 1] - q2s[yy + 1])

    def compute(field):
        vel_edges(field, inner_rows)

        columns(lambda yys: vel_columns(field, yys), 3, NY - 2, 5)
        if field == 0:
            y_halo_early(1)
        y_halo_recv(field)
        vel_edges(field, every)
        true = me.n >= 0
        vel_columns(field, [1, 2, NY + 1, NY + 2], [me.n > 0, true, true, me.n < 7])

        def back(i):
            for c2 in range(2):
                k = i * 2 + c2
                half_of = rest(me.c + k // 8 + field, 2)
                p, slab = half_of * 8 + k % 8, (me.n * 2 + half_of, k % 8)
                for half in range(2):
                    rs[field, p, pl.ds(half * NX, NX), :] = adjoint(2 * p + 2 + half)
                start_any(
                    rs.at[field, p], rv.at[field, me.w], ret_send.at[field], ret_recv.at[field], slab
                )

        for i in range(8):
            back(i)

    def arrive(field):
        await_bytes(rb.at[field, pl.ds(2 * MSG, 14 * MSG), :], leg2_recv.at[field, 1])

    for field in range(2):
        dens_gradient(field)
    arrive(0)
    compute(0)
    arrive(1)
    compute(1)

    for field in range(2):
        dens_edges(field)

        columns(lambda yys: dens_columns(field, yys), 2, NY, 4)
        dens_columns(field, [1, NY + 2])

        def keep_force(y, _):
            for k in range(4):
                at = pl.ds(pl.multiple_of((4 * y + k) * NX, 8), NX)
                df[field, at, :] = adjoint(4 * y + k + 2)
            return 0

        lax.fori_loop(0, NY // 4, keep_force, 0)

    for field in range(2):

        def turn(x, _):
            dens_out[field, x] = df[field, pl.ds(x, NY, stride=NX), :]
            return 0

        lax.fori_loop(0, NX, turn, 0)

    def seis_rows(i, _):
        for level in range(4):
            t = jnp.tanh(sl[level, pl.ds(pl.multiple_of(PAD + i * 32, 8), 32), :])
            scale = vel_coeff[level] * (1.0 / 16.0)
            seis_slope[level, pl.ds(pl.multiple_of(i * 32, 8), 32), :] = scale * (1.0 - t * t)
        return 0

    lax.fori_loop(0, slab_rows // 32, seis_rows, 0)

    for field in range(2):

        await_bytes(rv.at[field], ret_recv.at[field])

        def finish(block, _):
            for half in range(2):
                vel_out[field, pl.ds(block * 2 * NX + half, NX, stride=2), :] = rv[
                    field, block, pl.ds(half * NX, NX), :
                ]
            return 0

        lax.fori_loop(0, 16, finish, 0)

    for here, copy, _, _ in dens_halos:

        @pl.when(here)
        def _():
            copy.wait_send()

    for field in range(2):
        y_halo_sent(field)

        await_bytes(sb.at[field, pl.ds(0, 6)], leg1_send.at[field])
        await_bytes(rb.at[field, pl.ds(0, 15 * MSG), :], leg2_send.at[field])
        await_bytes(rs.at[field, pl.ds(0, 15)], ret_send.at[field])

        @pl.when(me.mid == 0)
        def _():
            await_bytes(sb.at[field, 0], leg1_send.at[field])

        @pl.when(me.mid == 1)
        def _():
            await_bytes(rb.at[field, pl.ds(0, MSG), :], leg2_send.at[field])

        @pl.when(me.w // 2 != me.n)
        def _():
            await_bytes(rs.at[field, 0], ret_send.at[field])


def chain_kernel(
    steps,
    dens_force,
    vel_force,
    grav_slope,
    seis_slope,
    grav_gradient,
    grav_curvature,
    seis_gradient,
    seis_curvature,
    brick_outs,
    slab_outs,
    sems,
):
    parts = (
        (grav_slope, dens_force, (grav_gradient, grav_curvature), brick_outs, 0),
        (seis_slope, vel_force, (seis_gradient, seis_curvature), slab_outs, 2),
    )

    def step(i, _):
        for slope, force, outs, made, sem in parts:
            rows = slope.shape[1] // steps
            here = pl.ds(i * rows, rows)
            for level in range(4):
                factor = slope[level, here]
                for number in range(2):
                    made[number, level, here] = factor * force[number, here]
            for number in range(2):
                pltpu.make_async_copy(
                    made.at[number, :, here], outs[number].at[:, here], sems.at[sem + number]
                ).start()
        return 0

    lax.fori_loop(0, steps, step, 0)
    for _, _, outs, made, sem in parts:
        for number in range(2):
            pltpu.make_async_copy(made.at[number], outs[number], sems.at[sem + number]).wait()


def shards(
    grav_levels,
    grav_step,
    seis_levels,
    seis_step,
    unit_labels,
    dens_index,
    vel_index,
    dens_table,
    vel_table,
):
    levels, nx, ny, nz = grav_levels.shape
    slab_x, slab_y = seis_levels.shape[1:3]
    rows = slab_x * slab_y
    seis_rows = seis_levels.reshape(levels, rows, nz)
    step_rows = seis_step.reshape(levels, rows, nz)
    tables = (unit_labels, dens_index, vel_index, dens_table, vel_table)
    hbm = pl.BlockSpec(memory_space=pltpu.HBM)
    vmem = pl.BlockSpec(memory_space=pltpu.VMEM)
    f32 = jnp.float32
    dma = pltpu.SemaphoreType.DMA
    brick_shape = jax.ShapeDtypeStruct(grav_levels.shape, f32)
    slab_shape = jax.ShapeDtypeStruct(seis_rows.shape, f32)
    forces = pl.pallas_call(
        forces_kernel,
        out_shape=(
            jax.ShapeDtypeStruct((2, nx, ny, nz), f32),
            jax.ShapeDtypeStruct((2, rows, nz), f32),
            brick_shape,
            slab_shape,
        ),
        in_specs=[hbm] * 9,
        out_specs=(vmem,) * 4,
        scratch_shapes=[
            *(pltpu.SMEM(table.shape, table.dtype) for table in tables),
            pltpu.VMEM((levels, nx, ny, nz), f32),
            pltpu.VMEM((levels, nx, ny, nz), f32),
            pltpu.VMEM((levels, rows + 4 * PAD, nz), f32),
            pltpu.VMEM((levels, rows + 4 * PAD, nz), f32),
            pltpu.VMEM((2, 8, 2 * MSG, nz), f32),
            pltpu.VMEM((2, 8, 2 * MSG, nz), f32),
            pltpu.VMEM((2, COLS, nz), f32),
            pltpu.VMEM((2, COLS, nz), f32),
            pltpu.VMEM((2, 4 * NY, nz), f32),
            pltpu.VMEM((2, 4 * NY, nz), f32),
            pltpu.VMEM((2, 4 * NX, nz), f32),
            pltpu.VMEM((2, 4 * NX, nz), f32),
            pltpu.VMEM((4, 8, nz), f32),
            pltpu.VMEM((4, 8, nz), f32),
            pltpu.VMEM((4, 3, NY + 4, NX, nz), f32),
            pltpu.VMEM((4, 3, 2, NY, nz), f32),
            pltpu.VMEM((2, 3, NY + 4, NX, nz), f32),
            pltpu.VMEM((2, 3, 2, NY, nz), f32),
            pltpu.VMEM((2, NY, nz), f32),
            pltpu.VMEM((5, NX + 16, nz), f32),
            pltpu.VMEM((NY + 4, NX, nz), f32),
            pltpu.VMEM((NY + 4, NX, nz), f32),
            pltpu.VMEM((2, NY * NX, nz), f32),
            pltpu.VMEM((2, 16, 2 * NX, nz), f32),
            pltpu.VMEM((2, 16, 2 * NX, nz), f32),
            dma((9,)),
            dma((2,)),
            dma((2, 8)),
            dma((2,)),
            dma((2, 3)),
            dma((2,)),
            dma((2,)),
            dma((2,)),
            dma((2,)),
            dma((4,)),
            dma((4,)),
            dma((2, 2)),
            dma((2, 2)),
            dma((2,)),
            dma((2,)),
        ],
        compiler_params=pltpu.CompilerParams(
            collective_id=0, has_side_effects=True, vmem_limit_bytes=42 << 20
        ),
        name="forces",
    )(*(pltpu.with_memory_space_constraint(v, pltpu.HBM) for v in (grav_levels, grav_step, seis_rows, step_rows, *tables)))

    outs = pl.pallas_call(
        functools.partial(chain_kernel, 8),
        out_shape=(brick_shape, brick_shape, slab_shape, slab_shape),
        in_specs=[vmem] * 4,
        out_specs=(hbm,) * 4,
        scratch_shapes=[
            pltpu.VMEM((2, *brick_shape.shape), f32),
            pltpu.VMEM((2, *slab_shape.shape), f32),
            dma((4,)),
        ],
        compiler_params=pltpu.CompilerParams(vmem_limit_bytes=32 << 20),
        name="chain",
    )(*forces)
    return (
        outs[0],
        outs[1],
        outs[2].reshape(seis_levels.shape),
        outs[3].reshape(seis_levels.shape),
    )


def solution(mesh):
    placed = (
        P(None, "wide", "narrow", None),
        P(None, "wide", "narrow", None),
        P(None, None, ("wide", "narrow"), None),
        P(None, None, ("wide", "narrow"), None),
        P(),
        P(),
        P(),
        P(),
        P(),
    )
    return jax.shard_map(
        shards,
        mesh=mesh,
        in_specs=placed,
        out_specs=placed[:4],
        check_vma=False,
    )
```
